256 devices in a mesh: lon: 16 (over x_lo, z), lat: 8 (over y, x_hi), ens: 2 (over core).
Axes of the slice: x: 4 (x_hi: 2, x_lo: 2; x = x_hi * 2 + x_lo), y: 4, z: 8, core: 2. Of those that a mesh axis runs over, the one named last changes fastest.
Arguments:
- inputs: bfloat16 [2, 2, 144, 384, 192], P('ens', None, 'lat', 'lon'), may hold values from -6 to 6
- cotangent: bfloat16 [2, 2, 144, 384, 192], P('ens', None, 'lat', 'lon'), may hold values from -6 to 6
- mask_ids: int32 [2, 144, 384], P(None, 'lat', 'lon'), may hold values from 0 to 3
- norm_gain: float32 [192], replicated, may hold values from 0.5 to 1.5
- project_in: bfloat16 [192, 576], replicated, may hold values from -0.4375 to 0.4375
- project_out: bfloat16 [192, 192], replicated, may hold values from -0.4375 to 0.4375
- bias_table: float32 [24, 6, 3312], replicated, may hold values from -4 to 265
Outputs:
- block_out: bfloat16 [2, 2, 144, 384, 192], P('ens', None, 'lat', 'lon')
- inputs_grad: bfloat16 [2, 2, 144, 384, 192], P('ens', None, 'lat', 'lon')
- project_in_grad: float32 [192, 576], replicated
- project_out_grad: float32 [192, 192], replicated
- gain_grad: float32 [192], replicated
- table_grad: float32 [24, 6, 3312], replicated
The draws below stay inside these ranges and needn't reach their ends.
All inputs are finite; a program needn't handle non-finite values.
Results may differ from the reference program's by a relative error of at most 0.014.
Values may be sent and summed in bfloat16 or wider, within the bound.
No kernel may reach another device: no remote copies, remote signals or barrier semaphores. Data moves between devices by JAX's collectives and lax.ppermute only.
A program may use at most 128 MiB of HBM per device.

```python
import jax
import jax.numpy as jnp
from jax import lax

C = 192
HEADS = 6
WL = 2
WLAT = 6
WLON = 12
PL = 2
MEMBERS = 2
NLAT = 144
NLON = 384
NWL = 1
NWLAT = 24
TYPES = 24


def draw_bias_table(key, part):
    key = jax.random.fold_in(key, 7)
    key_one = jax.random.fold_in(key, 0)
    shape = (TYPES, HEADS, WL, WL, WLAT, WLAT, 2 * WLON - 1)
    full = jnp.clip(jax.random.normal(key_one, shape, jnp.float32), -4.0, 4.0)
    return full.reshape(TYPES, HEADS, WL * WL * WLAT * WLAT * (2 * WLON - 1))


def set_ends(values, key, smallest, high):
    dims = values.shape
    index_at = [jax.random.randint(jax.random.fold_in(key, axis), (), 0, dims[axis]) for axis in range(len(dims))]
    values = values.at[tuple(index_at)].set(smallest)
    longest = dims.index(max(dims))
    index_at[longest] = (index_at[longest] + 1) % dims[longest]
    return values.at[tuple(index_at)].set(high)


def shard_levels(own_key, extent, cuts, least, largest):
    level, own = 1.0, jax.random.fold_in(own_key, 6)
    for dim, parts in cuts:
        draws = jnp.exp(jax.random.uniform(jax.random.fold_in(own, dim), (parts,), jnp.float32, least / len(cuts), largest / len(cuts)))
        level = level * jnp.repeat(draws, extent[dim] // parts).reshape([-1 if axis == dim else 1 for axis in range(len(extent))])
    return level


def bell_draw(stream_key, dims, deviation, reach, cuts=(), kind=jnp.bfloat16):
    gain = shard_levels(stream_key, dims, cuts, -0.22, 0.18) if cuts else 1.0
    entries = jax.random.normal(stream_key, dims, jnp.float32) * deviation * gain
    return jnp.minimum(jnp.maximum(entries, -reach), reach).astype(kind)


def setup_inputs(seed: int = 0) -> dict:
    keys = jax.random.split(jax.random.key(seed), 8)
    inputs = bell_draw(keys[0], (MEMBERS, PL, NLAT, NLON, C), 1.0, 6.0, ((0, 2), (2, 8), (3, 16)))
    cotangent = bell_draw(keys[1], (MEMBERS, PL, NLAT, NLON, C), 1.0, 6.0, ((0, 2), (2, 8), (3, 16)))
    mask_ids = set_ends(jax.random.randint(keys[2], (PL, NLAT, NLON), 0, 4), jax.random.fold_in(keys[2], 1), 0, 3).astype(jnp.int32)
    norm_gain = jnp.clip(1.0 + 0.1 * jax.random.normal(keys[3], (C,), jnp.float32), 0.5, 1.5)
    project_in = bell_draw(keys[4], (C, 3 * C), C ** -0.5, 0.4375)
    project_out = bell_draw(keys[5], (C, C), C ** -0.5, 0.4375)
    bias_table = draw_bias_table(jax.random.fold_in(keys[7], 71), 0)
    return dict(inputs=inputs, cotangent=cotangent, mask_ids=mask_ids, norm_gain=norm_gain, project_in=project_in, project_out=project_out, bias_table=bias_table)


EPS = 1e-05

def offset_table(width):
    position = jnp.arange(width, dtype=jnp.int32)
    delta = position[:, None] - position[None, :] + (width - 1)
    return (delta[None] == jnp.arange(2 * width - 1, dtype=jnp.int32)[:, None, None]).astype(jnp.float32)

def expand_bias(compact):
    lead = compact.shape[:-1]
    count = len(lead)
    shaped = compact.reshape(lead + (WL, WL, WLAT, WLAT, 2 * WLON - 1))
    full = jnp.einsum('...abcdx,xef->...abcdef', shaped, offset_table(WLON), precision=lax.Precision.HIGHEST)
    order = tuple(range(count)) + (count, count + 2, count + 4, count + 1, count + 3, count + 5)
    points = WL * WLAT * WLON
    return full.transpose(order).reshape(lead + (points, points))

def compress_bias(full):
    lead = full.shape[:-2]
    count = len(lead)
    shaped = full.reshape(lead + (WL, WLAT, WLON, WL, WLAT, WLON))
    order = tuple(range(count)) + (count, count + 3, count + 1, count + 4, count + 2, count + 5)
    shaped = shaped.transpose(order)
    small = jnp.einsum('...abcdef,xef->...abcdx', shaped, offset_table(WLON), precision=lax.Precision.HIGHEST)
    return small.reshape(lead + (-1,))

def to_windows(volume, win_depth, win_rows, win_cols):
    members, levels, lat_rows, lon_cols, channels = volume.shape
    shaped = volume.reshape(members, levels // win_depth, win_depth, lat_rows // win_rows, win_rows, lon_cols // win_cols, win_cols, channels)
    shaped = shaped.transpose(0, 1, 3, 5, 2, 4, 6, 7)
    return shaped.reshape(members, levels // win_depth, lat_rows // win_rows, lon_cols // win_cols, win_depth * win_rows * win_cols, channels)

def from_windows(window_set, win_depth, win_rows, win_cols):
    members, lev_win, lat_win, lon_win, points, channels = window_set.shape
    shaped = window_set.reshape(members, lev_win, lat_win, lon_win, win_depth, win_rows, win_cols, channels)
    shaped = shaped.transpose(0, 1, 4, 2, 5, 3, 6, 7)
    return shaped.reshape(members, lev_win * win_depth, lat_win * win_rows, lon_win * win_cols, channels)

def window_pass(seq_in, seq_cot, region, bias_win, project_in, project_out):
    f32 = jnp.float32
    bf16 = jnp.bfloat16
    num_win, points, channels = seq_in.shape
    head_num = bias_win.shape[1]
    head_dim = channels // head_num
    factor = head_dim ** (-0.5)
    weight_in = project_in.astype(f32)
    weight_out = project_out.astype(f32)
    triple = jnp.einsum('npc,cf->npf', seq_in.astype(f32), weight_in).astype(bf16)
    triple = triple.reshape(num_win, points, 3, head_num, head_dim)
    queries, key_vec, val_vec = (triple[:, :, 0], triple[:, :, 1], triple[:, :, 2])
    scores = jnp.einsum('nqhd,nkhd->nhqk', queries.astype(f32), key_vec.astype(f32)) * factor + bias_win
    allowed = (region[:, :, None] == region[:, None, :])[:, None]
    scores = jnp.where(allowed, scores, -jnp.inf)
    peak_val = lax.optimization_barrier(jnp.max(scores, axis=-1, keepdims=True))
    raised = jnp.exp(scores - peak_val)
    prob_full = raised / lax.optimization_barrier(jnp.sum(raised, axis=-1, keepdims=True))
    prob_low = prob_full.astype(bf16)
    mixed = jnp.einsum('nhqk,nkhd->nqhd', prob_low.astype(f32), val_vec.astype(f32)).astype(bf16)
    mixed = mixed.reshape(num_win, points, channels)
    attended = jnp.einsum('npc,cd->npd', mixed.astype(f32), weight_out).astype(bf16)
    out_grad = jnp.einsum('npc,npd->cd', mixed.astype(f32), seq_cot.astype(f32))
    grad_mixed = jnp.einsum('npd,cd->npc', seq_cot.astype(f32), weight_out).astype(bf16)
    grad_mixed = grad_mixed.reshape(num_win, points, head_num, head_dim)
    grad_probs = jnp.einsum('nqhd,nkhd->nhqk', grad_mixed.astype(f32), val_vec.astype(f32))
    grad_value = jnp.einsum('nhqk,nqhd->nkhd', prob_low.astype(f32), grad_mixed.astype(f32)).astype(bf16)
    grad_scores = prob_full * (grad_probs - lax.optimization_barrier(jnp.sum(prob_full * grad_probs, axis=-1, keepdims=True)))
    grad_low = grad_scores.astype(bf16).astype(f32)
    grad_query = (jnp.einsum('nhqk,nkhd->nqhd', grad_low, key_vec.astype(f32)) * factor).astype(bf16)
    grad_key = (jnp.einsum('nhqk,nqhd->nkhd', grad_low, queries.astype(f32)) * factor).astype(bf16)
    grad_triple = jnp.stack([grad_query, grad_key, grad_value], axis=2).reshape(num_win, points, 3 * channels)
    in_grad = jnp.einsum('npc,npf->cf', seq_in.astype(f32), grad_triple.astype(f32))
    grad_seq = jnp.einsum('npf,cf->npc', grad_triple.astype(f32), weight_in).astype(bf16)
    return (attended, grad_seq, in_grad, out_grad, grad_scores)

def reference(inputs, cotangent, mask_ids, norm_gain, project_in, project_out, bias_table):
    f32 = jnp.float32
    values = inputs.astype(f32)
    average = lax.optimization_barrier(jnp.mean(values, axis=-1, keepdims=True))
    center = values - average
    inverse = lax.rsqrt(lax.optimization_barrier(jnp.mean(center * center, axis=-1, keepdims=True)) + EPS)
    normal_part = center * inverse
    normed = (normal_part * norm_gain).astype(jnp.bfloat16)
    moves = (-(WL // 2), -(WLAT // 2), -(WLON // 2))
    shifted = jnp.roll(normed, moves, axis=(1, 2, 3))
    shifted_cot = jnp.roll(cotangent, moves, axis=(1, 2, 3))
    window_set = to_windows(shifted, WL, WLAT, WLON)
    cot_set = to_windows(shifted_cot, WL, WLAT, WLON)
    regions = to_windows(mask_ids[None, :, :, :, None], WL, WLAT, WLON)[0, :, :, :, :, 0]
    table_rows = bias_table.reshape(NWL, NWLAT, bias_table.shape[1], bias_table.shape[2])

    def one_band(index):
        band_tiles = lax.dynamic_index_in_dim(window_set, index, 2, keepdims=False)
        band_cot = lax.dynamic_index_in_dim(cot_set, index, 2, keepdims=False)
        band_region = lax.dynamic_index_in_dim(regions, index, 1, keepdims=False)
        compact = lax.dynamic_index_in_dim(table_rows, index, 1, keepdims=False)
        band_bias = expand_bias(compact)
        members, lev_win, lon_win, points, channels = band_tiles.shape
        num_win = members * lev_win * lon_win
        region_rows = jnp.broadcast_to(band_region[None], (members, lev_win, lon_win, points)).reshape(num_win, points)
        tail = band_bias.shape[1:]
        bias_rows = jnp.broadcast_to(band_bias[None, :, None], (members, lev_win, lon_win) + tail).reshape((num_win,) + tail)
        attended, grad_seq, in_grad, out_grad, grad_scores = window_pass(band_tiles.reshape(num_win, points, channels), band_cot.reshape(num_win, points, channels), region_rows, bias_rows, project_in, project_out)
        band_sum = compress_bias(lax.optimization_barrier(jnp.sum(grad_scores.reshape((members, lev_win, lon_win) + tail), axis=(0, 2))))
        return (attended.reshape(band_tiles.shape), grad_seq.reshape(band_tiles.shape), in_grad, out_grad, band_sum)
    attended, grad_seq, in_grads, out_grads, band_sums = lax.map(one_band, jnp.arange(NWLAT, dtype=jnp.int32))
    attended = from_windows(jnp.moveaxis(attended, 0, 2), WL, WLAT, WLON)
    grad_seq = from_windows(jnp.moveaxis(grad_seq, 0, 2), WL, WLAT, WLON)
    backs = (WL // 2, WLAT // 2, WLON // 2)
    attended = jnp.roll(attended, backs, axis=(1, 2, 3))
    grad_normed = jnp.roll(grad_seq, backs, axis=(1, 2, 3))
    block_out = (values + attended.astype(f32)).astype(jnp.bfloat16)
    table_grad = jnp.transpose(band_sums, (1, 0, 2, 3)).reshape(bias_table.shape)
    grad_wide = grad_normed.astype(f32)
    scaled = grad_wide * norm_gain
    gain_grad = lax.optimization_barrier(jnp.sum(grad_wide * normal_part, axis=(0, 1, 2, 3)))
    grad_part = inverse * (scaled - lax.optimization_barrier(jnp.mean(scaled, axis=-1, keepdims=True)) - normal_part * lax.optimization_barrier(jnp.mean(scaled * normal_part, axis=-1, keepdims=True)))
    inputs_grad = (cotangent.astype(f32) + grad_part).astype(jnp.bfloat16)
    return (block_out, inputs_grad, lax.optimization_barrier(jnp.sum(in_grads, axis=0)), lax.optimization_barrier(jnp.sum(out_grads, axis=0)), gain_grad, table_grad)
```

```python
import functools

import jax
import jax.numpy as jnp
from jax import lax
from jax.experimental import pallas as pl
from jax.experimental.pallas import tpu as pltpu
from jax.sharding import PartitionSpec as P

WL, WLAT, WLON = 2, 6, 12
AB = WL * WLAT
POINTS = AB * WLON
SPAN = 2 * WLON - 1
EPS = 1e-05
F32, BF16, I32 = jnp.float32, jnp.bfloat16, jnp.int32
C, HEADS, HD = 192, 6, 32
FACTOR = HD ** (-0.5)
TAB = 3
ENTRIES = AB * AB * SPAN
LANE_BLOCKS = -(-ENTRIES // 128)
CHUNK = 64
G_ROWS = 40
T_ROWS = 16
SHARD = 176
VMEM = pltpu.CompilerParams(vmem_limit_bytes=56 * 2**20)


def dot(a, b, ca, cb):
    return lax.dot_general(a, b, (((ca,), (cb,)), ((), ())), preferred_element_type=F32)


def iota(shape, dim):
    return lax.broadcasted_iota(I32, shape, dim)


def segments():
    for ab_p in range(AB):
        a_p, b_p = divmod(ab_p, WLAT)
        for ab_r in range(AB):
            a_r, b_r = divmod(ab_r, WLAT)
            yield ab_p, ab_r, (((a_p * WL + a_r) * WLAT + b_p) * WLAT + b_r) * SPAN


def toeplitz(target, c):
    return (iota((384, POINTS), 0) == target + (WLON - 1 - c)).astype(BF16)


def expand_kernel(table_ref, target_ref, order_ref, bias_ref, rows_ref):
    rows_ref[...] = jnp.zeros_like(rows_ref)
    for t in range(TAB):
        for ab_p, ab_r, start in segments():
            rows_ref[t, ab_r * 8 : ab_r * 8 + HEADS, ab_p * SPAN : (ab_p + 1) * SPAN] = table_ref[
                t, :, start : start + SPAN
            ]
    order = order_ref[...]
    target = target_ref[...]
    pieces = []
    rest = [rows_ref[t] for t in range(TAB)]
    for _ in range(3):
        low = [r.astype(BF16) for r in rest]
        rest = [r - p.astype(F32) for r, p in zip(rest, low)]
        pieces.append(jnp.concatenate([dot(order, p, 1, 0).astype(BF16) for p in low], axis=0))
    for c in range(WLON):
        pick = toeplitz(target, c)
        full = dot(pieces[0], pick, 1, 0) + (dot(pieces[1], pick, 1, 0) + dot(pieces[2], pick, 1, 0))
        for th in range(TAB * HEADS):
            bias_ref[th, c * AB : (c + 1) * AB, :] = full[th * 16 : th * 16 + AB, :]


def main_kernel(
    ens_ref, x_ref, y_ref, lon_ref, lat_ref, cor_ref, region_ref, gain_ref, win_ref, win_t_ref, wout_ref,
    wout_t_ref, bias_ref, place_ref, target_ref, order_ref,
    out_ref, ig_ref, lon_out, lat_out, cor_out, keep_ref, send_ref,
    ext, grads, outer, gain_acc, dbias, blocks, rows, flat_t, flat, chunks,
):
    for k, ref in enumerate((x_ref, y_ref)):
        ext[k, :, 0:18, 0:24, :] = ref[...].astype(F32)
        ext[k, :, 0:18, 24:32, :] = lon_ref[k].astype(F32)
        ext[k, :, 18:21, 0:24, :] = lat_ref[k].astype(F32)
        ext[k, :, 18:21, 24:32, :] = cor_ref[k].astype(F32)
    grads[...] = jnp.zeros_like(grads)
    outer[...] = jnp.zeros_like(outer)
    gain_acc[...] = jnp.zeros_like(gain_acc)
    gain = gain_ref[...]
    place = place_ref[...]

    def row(v, carry):
        span = pl.ds(6 * v + 3, 6)
        xw = ext[0, :, span].reshape(384, C).astype(BF16)
        yw = ext[1, :, span].reshape(384, C).astype(BF16)
        out_w = jnp.zeros((384, C), F32)
        ig_w = jnp.zeros((384, C), F32)
        for w in range(2):
            pick = (iota((384, POINTS), 0) == place + WLON * w).astype(BF16)
            xt = dot(xw, pick, 0, 0)
            ct32 = dot(yw, pick, 0, 0)
            ct = ct32.astype(BF16)
            center = xt - jnp.mean(xt, axis=0, keepdims=True)
            inverse = lax.rsqrt(jnp.mean(center * center, axis=0, keepdims=True) + EPS)
            part = center * inverse
            normed = (part * gain).astype(BF16)
            triple = dot(win_t_ref[...], normed, 1, 0).astype(BF16)
            grad_mixed = dot(wout_ref[...], ct, 1, 0).astype(BF16)
            ids = region_ref[v, w]
            member = (iota((8, POINTS), 0) == ids).astype(BF16)
            barred = (dot(member, member, 0, 0) - 1.0) * 1e30
            mixed, g_q, g_k, g_v = [], [], [], []
            for h in range(HEADS):
                lo, hi = h * HD, (h + 1) * HD
                q, k, val = triple[lo:hi], triple[C + lo : C + hi], triple[2 * C + lo : 2 * C + hi]
                gm = grad_mixed[lo:hi]
                scores = dot(k, q, 0, 0) * FACTOR + (bias_ref[v * HEADS + h] + barred)
                raised = jnp.exp(scores - jnp.max(scores, axis=0, keepdims=True))
                prob = raised * (1.0 / jnp.sum(raised, axis=0, keepdims=True))
                low = prob.astype(BF16)
                mixed.append(dot(val, low, 1, 0))
                g_prob = dot(val, gm, 0, 0)
                g_v.append(dot(gm, low, 1, 1))
                g_score = prob * (g_prob - jnp.sum(prob * g_prob, axis=0, keepdims=True))
                if w == 0:
                    dbias[v * HEADS + h] = g_score
                else:
                    dbias[v * HEADS + h] += g_score
                g_low = g_score.astype(BF16)
                g_q.append(dot(k, g_low, 1, 0) * FACTOR)
                g_k.append(dot(q, g_low, 1, 1) * FACTOR)
            mixed = jnp.concatenate(mixed, axis=0).astype(BF16)
            attended = dot(wout_t_ref[...], mixed, 1, 0).astype(BF16)
            outer[...] += dot(mixed, ct, 1, 1)
            g_triple = jnp.concatenate(g_q + g_k + g_v, axis=0).astype(BF16)
            grads[:, : 3 * C] += dot(normed, g_triple, 1, 1)
            wide = dot(win_ref[...], g_triple, 1, 0).astype(BF16).astype(F32)
            block = (xt + attended.astype(F32)).astype(BF16)
            gain_acc[...] += wide * part
            scaled = wide * gain
            grad_part = inverse * (
                scaled
                - jnp.mean(scaled, axis=0, keepdims=True)
                - part * jnp.mean(scaled * part, axis=0, keepdims=True)
            )
            in_grad = (ct32 + grad_part).astype(BF16)
            out_w = out_w + dot(pick, block, 1, 1)
            ig_w = ig_w + dot(pick, in_grad, 1, 1)
        ext[0, :, span] = out_w.reshape(2, 6, 32, C)
        ext[1, :, span] = ig_w.reshape(2, 6, 32, C)
        return carry

    lax.fori_loop(0, TAB, row, 0)
    for k, ref in enumerate((out_ref, ig_ref)):
        ext[k, :, 0:3] = jnp.zeros((2, 3, 32, C), F32)
        ref[...] = ext[k, :, 0:18, 0:24, :].astype(BF16)
        lon_out[k] = ext[k, :, 0:18, 24:32, :].astype(BF16)
        lat_out[k] = ext[k, :, 18:21, 0:24, :].astype(BF16)
        cor_out[k] = ext[k, :, 18:21, 24:32, :].astype(BF16)

    blocks[...] = jnp.zeros_like(blocks)
    total = jnp.zeros((TAB * HEADS * 16, 384), F32)
    for c in range(WLON):
        for th in range(TAB * HEADS):
            blocks[th * 16 : th * 16 + AB, :] = dbias[th, c * AB : (c + 1) * AB, :]
        total = total + dot(blocks[...].astype(BF16), toeplitz(target_ref[...], c), 1, 1)
    flat_t[...] = jnp.zeros_like(flat_t)
    for t in range(TAB):
        rows[...] = dot(order_ref[...], total[t * 96 : (t + 1) * 96].astype(BF16), 0, 0)
        for ab_p, ab_r, start in segments():
            flat_t[t * 8 : t * 8 + 8, start : start + SPAN] = rows[
                ab_r * 8 : ab_r * 8 + 8, ab_p * SPAN : (ab_p + 1) * SPAN
            ]
    flat[...] = jnp.zeros_like(flat)
    for block in range(LANE_BLOCKS):
        for t in range(TAB):
            at = (block * TAB + t) * HEADS
            flat[at : at + HEADS, :] = flat_t[t * 8 : t * 8 + HEADS, block * 128 : (block + 1) * 128]

    chunks[...] = jnp.zeros_like(chunks)
    grads[:, 3 * C :] = outer[...]
    tile = 0
    for group in range(C // 8):
        for block in range(C * 4 // 128):
            chunk, slot = divmod(tile, G_ROWS // 8)
            chunks[chunk // 16, chunk % 16, slot * 8 : slot * 8 + 8, :] = grads[
                group * 8 : group * 8 + 8, block * 128 : (block + 1) * 128
            ]
            tile += 1
    for chunk in range(32):
        chunks[chunk // 16, chunk % 16, G_ROWS : G_ROWS + T_ROWS, :] = flat[chunk * T_ROWS : (chunk + 1) * T_ROWS]
    rest = gain_acc[...]
    gain_row = jnp.zeros((8, C), F32)
    for _ in range(3):
        low = rest.astype(BF16)
        rest = rest - low.astype(F32)
        gain_row = gain_row + dot(jnp.ones((8, POINTS), BF16), low, 1, 1)
    chunks[1, 13, 0:1, :] = gain_row[0:1, 0:128]
    chunks[1, 13, 1:2, 0:64] = gain_row[0:1, 128:192]
    me = ens_ref[0]
    keep_ref[...] = chunks[me]
    send_ref[...] = chunks[1 - me].astype(BF16)


def over_lon_kernel(got_ref, out_ref):
    total = jnp.sum(got_ref[...].astype(F32), axis=0).astype(BF16)
    for k in range(out_ref.shape[0]):
        out_ref[k] = total


def over_lat_kernel(got_ref, out_ref):
    got = got_ref[...].astype(F32)
    total = jnp.sum(got[:, : G_ROWS + 8], axis=0)
    shard = jnp.concatenate([total] + [got[k, G_ROWS : G_ROWS + T_ROWS] for k in range(8)], axis=0).astype(BF16)
    for k in range(out_ref.shape[0]):
        out_ref[k] = shard


def final_kernel(ens_ref, mine_ref, other_ref, order_ref, in_ref, outer_ref, gain_ref, table_ref, both, tables, grads, full):
    me = ens_ref[0]
    both[me] = mine_ref[...].astype(F32)
    both[1 - me] = other_ref[...].astype(F32)
    tile = 0
    for group in range(C // 8):
        for block in range(C * 4 // 128):
            chunk, slot = divmod(tile, G_ROWS // 8)
            grads[group * 8 : group * 8 + 8, block * 128 : (block + 1) * 128] = both[
                chunk // 16, chunk % 16, slot * 8 : slot * 8 + 8, :
            ]
            tile += 1
    in_ref[...] = grads[:, 0 : 3 * C]
    outer_ref[...] = grads[:, 3 * C :]
    gain_ref[0:1, 0:128] = both[1, 13, 0:1, :]
    gain_ref[0:1, 128:192] = both[1, 13, 1:2, 0:64]
    for lat in range(8):
        for chunk in range(32):
            tables[lat, chunk * T_ROWS : (chunk + 1) * T_ROWS, :] = both[
                chunk // 16, chunk % 16, G_ROWS + 8 + lat * T_ROWS : G_ROWS + 8 + (lat + 1) * T_ROWS, :
            ]
    count = TAB * HEADS
    for lat in range(8):
        for block in range(LANE_BLOCKS):
            full[lat * count : (lat + 1) * count, block * 128 : (block + 1) * 128] = tables[
                lat, block * count : (block + 1) * count, :
            ]
    ordered = dot(order_ref[...], full[...].astype(BF16), 1, 0)
    for h in range(HEADS):
        table_ref[h] = ordered[h * 24 : (h + 1) * 24, :ENTRIES]


def vmem(count):
    return [pl.BlockSpec(memory_space=pltpu.VMEM)] * count


SMEM = pl.BlockSpec(memory_space=pltpu.SMEM)


def struct(shape, dtype):
    return jax.ShapeDtypeStruct(shape, dtype)


def passed(x, axes, sizes, moves):
    total = [()]
    for size in sizes:
        total = [t + (i,) for t in total for i in range(size)]

    def number(index):
        n = 0
        for i, size in zip(index, sizes):
            n = n * size + i % size
        return n

    pairs = [(number(t), number(tuple(i + m for i, m in zip(t, moves)))) for t in total]
    return lax.ppermute(x, axes, pairs)


def halo(lon_strip, lat_strip, corner, by):
    n_lon, n_lat = lax.axis_size("lon"), lax.axis_size("lat")
    return (
        passed(lon_strip, "lon", (n_lon,), (by,)),
        passed(lat_strip, "lat", (n_lat,), (by,)),
        passed(corner, ("lon", "lat"), (n_lon, n_lat), (by, by)),
    )


def one_hot(index, width):
    return (index[:, None] == jnp.arange(width, dtype=I32)[None, :]).astype(BF16)


def local(inputs, cotangent, mask_ids, norm_gain, project_in, project_out, bias_table):
    x, y = inputs[0], cotangent[0]
    lat, ens = lax.axis_index("lat"), lax.axis_index("ens")
    pair = jnp.stack([x, y])
    strips = halo(pair[:, :, :, 0:8], pair[:, :, 0:3], pair[:, :, 0:3, 0:8], -1)

    p = jnp.arange(POINTS, dtype=I32)
    c_p, ab_p = p // AB, p % AB
    target = (ab_p * SPAN + c_p)[None]
    place = ((1 - ab_p // WLAT) * (WLAT * 32) + (ab_p % WLAT) * 32 + WLON // 2 + c_p)[None]
    n = jnp.arange(96, dtype=I32)
    order = one_hot(jnp.where(n % 16 < AB, (n % 16) * 8 + n // 16, -1), 96)
    table = lax.dynamic_slice_in_dim(bias_table, lat * TAB, TAB, 0)
    bias = pl.pallas_call(
        expand_kernel,
        out_shape=struct((TAB * HEADS, POINTS, POINTS), F32),
        in_specs=vmem(3),
        out_specs=vmem(1)[0],
        scratch_shapes=[pltpu.VMEM((TAB, 96, 384), F32)],
        compiler_params=VMEM,
    )(table, target, order)
    regions = mask_ids.reshape(WL, TAB, WLAT, 2, WLON).transpose(1, 3, 4, 0, 2).reshape(TAB, 2, 1, POINTS)
    me = ens.astype(I32).reshape(1)

    out, in_grad, lon_s, lat_s, cor_s, keep, send = pl.pallas_call(
        main_kernel,
        out_shape=(
            struct((2, 18, 24, C), BF16),
            struct((2, 18, 24, C), BF16),
            struct((2, 2, 18, 8, C), BF16),
            struct((2, 2, 3, 24, C), BF16),
            struct((2, 2, 3, 8, C), BF16),
            struct((16, CHUNK, 128), F32),
            struct((16, CHUNK, 128), BF16),
        ),
        in_specs=[SMEM] + vmem(15),
        out_specs=tuple(vmem(7)),
        scratch_shapes=[
            pltpu.VMEM((2, 2, 21, 32, C), F32),
            pltpu.VMEM((C, 4 * C), F32),
            pltpu.VMEM((C, C), F32),
            pltpu.VMEM((C, POINTS), F32),
            pltpu.VMEM((TAB * HEADS, POINTS, POINTS), F32),
            pltpu.VMEM((TAB * HEADS * 16, POINTS), F32),
            pltpu.VMEM((96, 384), F32),
            pltpu.VMEM((TAB * 8, LANE_BLOCKS * 128), F32),
            pltpu.VMEM((32 * T_ROWS, 128), F32),
            pltpu.VMEM((2, 16, CHUNK, 128), F32),
        ],
        compiler_params=VMEM,
    )(
        me, x, y, *strips, regions, norm_gain.reshape(C, 1), project_in, project_in.T, project_out, project_out.T,
        bias, place, target, order,
    )

    strips = halo(lon_s, lat_s, cor_s, 1)
    got = passed(send, "ens", (2,), (1,))
    part = (keep + got.astype(F32)).astype(BF16)
    part = lax.all_to_all(part, "lon", 0, 0, tiled=True)
    part = pl.pallas_call(
        over_lon_kernel,
        out_shape=struct((8, CHUNK, 128), BF16),
        in_specs=vmem(1),
        out_specs=vmem(1)[0],
        compiler_params=VMEM,
    )(part)
    part = lax.all_to_all(part, "lat", 0, 0, tiled=True)
    part = pl.pallas_call(
        over_lat_kernel,
        out_shape=struct((16, SHARD, 128), BF16),
        in_specs=vmem(1),
        out_specs=vmem(1)[0],
        compiler_params=VMEM,
    )(part)
    mine = lax.all_to_all(part, "lon", 0, 0, tiled=True)
    other = passed(mine, "ens", (2,), (1,))
    m = jnp.arange(144, dtype=I32)
    table_order = one_hot((m % 24) * HEADS + m // 24, 144)
    in_total, out_total, gain_total, table_total = pl.pallas_call(
        final_kernel,
        out_shape=(
            struct((C, 3 * C), F32),
            struct((C, C), F32),
            struct((1, C), F32),
            struct((HEADS, 24, ENTRIES), F32),
        ),
        in_specs=[SMEM] + vmem(3),
        out_specs=tuple(vmem(4)),
        scratch_shapes=[
            pltpu.VMEM((2, 16, SHARD, 128), F32),
            pltpu.VMEM((8, 32 * T_ROWS, 128), F32),
            pltpu.VMEM((C, 4 * C), F32),
            pltpu.VMEM((144, LANE_BLOCKS * 128), F32),
        ],
        compiler_params=VMEM,
    )(me, mine, other, table_order)

    both = jnp.stack([out, in_grad])
    lon_pad = jnp.pad(strips[0], ((0, 0), (0, 0), (0, 0), (0, 16), (0, 0)))
    lat_pad = jnp.pad(strips[1], ((0, 0), (0, 0), (0, 15), (0, 0), (0, 0)))
    cor_pad = jnp.pad(strips[2], ((0, 0), (0, 0), (0, 15), (0, 16), (0, 0)))
    both = both + lon_pad + lat_pad + cor_pad
    return (
        both[0][None],
        both[1][None],
        in_total,
        out_total,
        gain_total.reshape(C),
        table_total.transpose(1, 0, 2),
    )


def solution(mesh):
    return jax.shard_map(
        local,
        mesh=mesh,
        in_specs=(
            P("ens", None, "lat", "lon", None),
            P("ens", None, "lat", "lon", None),
            P(None, "lat", "lon"),
            P(),
            P(),
            P(),
            P(),
        ),
        out_specs=(
            P("ens", None, "lat", "lon", None),
            P("ens", None, "lat", "lon", None),
            P(),
            P(),
            P(),
            P(),
        ),
        check_vma=False,
    )
```

```python
import jax
import jax.numpy as jnp
from jax import lax
from jax.experimental import pallas as pl
from jax.experimental.pallas import tpu as pltpu
from jax.sharding import PartitionSpec as P

WL, WLAT, WLON = 2, 6, 12
AB = WL * WLAT
POINTS = AB * WLON
SPAN = 2 * WLON - 1
EPS = 1e-05
F32, BF16, I32 = jnp.float32, jnp.bfloat16, jnp.int32
C, HEADS, HD = 192, 6, 32
FACTOR = HD ** (-0.5)
TAB = 3
ENTRIES = AB * AB * SPAN
LANE_BLOCKS = -(-ENTRIES // 128)
CHUNK = 64
G_ROWS = 40
T_ROWS = 16
SHARD = 176


def dot(a, b, ca, cb):
    return lax.dot_general(a, b, (((ca,), (cb,)), ((), ())), preferred_element_type=F32)


def iota(shape, dim):
    return lax.broadcasted_iota(I32, shape, dim)


def segments():
    for ab_p in range(AB):
        a_p, b_p = divmod(ab_p, WLAT)
        for ab_r in range(AB):
            a_r, b_r = divmod(ab_r, WLAT)
            yield ab_p, ab_r, (((a_p * WL + a_r) * WLAT + b_p) * WLAT + b_r) * SPAN


def tokens():
    p = iota((1, POINTS), 1)
    c_p = (p * 21846) >> 18
    return c_p, p - c_p * AB


def toeplitz(c):
    c_p, ab_p = tokens()
    return (iota((384, POINTS), 0) == ab_p * SPAN + c_p + (WLON - 1 - c)).astype(BF16)


def heads_first():
    n = iota((96, 96), 0)
    return ((iota((96, 96), 1) == (n & 15) * 8 + (n >> 4)) & ((n & 15) < AB)).astype(BF16)


def strips_kernel(x_ref, y_ref, lon_ref, lat_ref, cor_ref):
    for k, ref in enumerate((x_ref, y_ref)):
        lon_ref[k] = ref[:, :, 0:8, :]
        lat_ref[k] = ref[:, 0:3, :, :]
        cor_ref[k] = ref[:, 0:3, 0:8, :]


def shadow_kernel(
    lat_ref, table_ref, gain_ref, win_ref, wout_ref, mask_ref,
    bias_ref, win_t_ref, wout_t_ref, gain_out, region_ref, own_ref, rows_ref, ids_ref,
):
    first = lat_ref[0] * TAB
    for t in range(TAB):
        for h in range(HEADS):
            own_ref[t, h : h + 1, :] = table_ref[h, pl.ds(first + t, 1), :]
    rows_ref[...] = jnp.zeros_like(rows_ref)
    for t in range(TAB):
        for ab_p, ab_r, start in segments():
            rows_ref[t, ab_r * 8 : ab_r * 8 + HEADS, ab_p * SPAN : (ab_p + 1) * SPAN] = own_ref[
                t, :, start : start + SPAN
            ]
    order = heads_first()
    pieces = []
    rest = [rows_ref[t] for t in range(TAB)]
    for _ in range(3):
        low = [r.astype(BF16) for r in rest]
        rest = [r - p.astype(F32) for r, p in zip(rest, low)]
        pieces.append(jnp.concatenate([dot(order, p, 1, 0).astype(BF16) for p in low], axis=0))
    for c in range(WLON):
        pick = toeplitz(c)
        full = dot(pieces[0], pick, 1, 0) + (dot(pieces[1], pick, 1, 0) + dot(pieces[2], pick, 1, 0))
        for th in range(TAB * HEADS):
            bias_ref[th, c * AB : (c + 1) * AB, :] = full[th * 16 : th * 16 + AB, :]
    win_t_ref[...] = win_ref[...].T
    wout_t_ref[...] = wout_ref[...].T
    column = jnp.broadcast_to(gain_ref[...], (8, C)).T
    gain_out[...] = jnp.broadcast_to(column[:, 0:1], (C, POINTS))
    ids_ref[...] = jnp.zeros_like(ids_ref)
    c_p, ab_p = tokens()
    for v in range(TAB):
        for b in range(WLAT):
            for a in range(WL):
                at = a * WLAT + b
                ids_ref[v, at : at + 1, 0:24] = mask_ref[v * WLAT + b, a : a + 1, :].astype(F32)
        for w in range(2):
            pick = (iota((128, POINTS), 0) == c_p + WLON * w).astype(BF16)
            spread = dot(ids_ref[v].astype(BF16), pick, 1, 0)
            own = jnp.where(iota((16, POINTS), 0) == ab_p, spread, 0.0)
            region_ref[v, w] = jnp.sum(own, axis=0, keepdims=True)


def main_kernel(
    ens_ref, x_ref, y_ref, lon_ref, lat_ref, cor_ref, region_ref, gain_ref, win_ref, win_t_ref, wout_ref,
    wout_t_ref, bias_ref,
    out_ref, ig_ref, lon_out, lat_out, cor_out, keep_ref, send_ref,
    ext, grads, outer, gain_acc, dbias, blocks, rows, flat_t, flat, chunks,
):
    for k, ref in enumerate((x_ref, y_ref)):
        ext[k, :, 0:18, 0:24, :] = ref[...].astype(F32)
        ext[k, :, 0:18, 24:32, :] = lon_ref[k].astype(F32)
        ext[k, :, 18:21, 0:24, :] = lat_ref[k].astype(F32)
        ext[k, :, 18:21, 24:32, :] = cor_ref[k].astype(F32)
    grads[...] = jnp.zeros_like(grads)
    outer[...] = jnp.zeros_like(outer)
    gain_acc[...] = jnp.zeros_like(gain_acc)
    gain = gain_ref[...]
    c_p, ab_p = tokens()
    level = jnp.where(ab_p >= WLAT, 1, 0)
    place = (1 - level) * (WLAT * 32) + (ab_p - level * WLAT) * 32 + WLON // 2 + c_p

    def row(v, carry):
        span = pl.ds(6 * v + 3, 6)
        xw = ext[0, :, span].reshape(384, C).astype(BF16)
        yw = ext[1, :, span].reshape(384, C).astype(BF16)
        out_w = jnp.zeros((384, C), F32)
        ig_w = jnp.zeros((384, C), F32)
        for w in range(2):
            pick = (iota((384, POINTS), 0) == place + WLON * w).astype(BF16)
            xt = dot(xw, pick, 0, 0)
            ct32 = dot(yw, pick, 0, 0)
            ct = ct32.astype(BF16)
            center = xt - jnp.mean(xt, axis=0, keepdims=True)
            inverse = lax.rsqrt(jnp.mean(center * center, axis=0, keepdims=True) + EPS)
            part = center * inverse
            normed = (part * gain).astype(BF16)
            triple = dot(win_t_ref[...], normed, 1, 0).astype(BF16)
            grad_mixed = dot(wout_ref[...], ct, 1, 0).astype(BF16)
            ids = region_ref[v, w]
            member = (iota((8, POINTS), 0).astype(F32) == ids).astype(BF16)
            barred = (dot(member, member, 0, 0) - 1.0) * 1e30
            mixed, g_q, g_k, g_v = [], [], [], []
            for h in range(HEADS):
                lo, hi = h * HD, (h + 1) * HD
                q, k, val = triple[lo:hi], triple[C + lo : C + hi], triple[2 * C + lo : 2 * C + hi]
                gm = grad_mixed[lo:hi]
                scores = dot(k, q, 0, 0) * FACTOR + (bias_ref[v * HEADS + h] + barred)
                raised = jnp.exp(scores - jnp.max(scores, axis=0, keepdims=True))
                prob = raised * (1.0 / jnp.sum(raised, axis=0, keepdims=True))
                low = prob.astype(BF16)
                mixed.append(dot(val, low, 1, 0))
                g_prob = dot(val, gm, 0, 0)
                g_v.append(dot(gm, low, 1, 1))
                g_score = prob * (g_prob - jnp.sum(prob * g_prob, axis=0, keepdims=True))
                if w == 0:
                    dbias[v * HEADS + h] = g_score
                else:
                    dbias[v * HEADS + h] += g_score
                g_low = g_score.astype(BF16)
                g_q.append(dot(k, g_low, 1, 0) * FACTOR)
                g_k.append(dot(q, g_low, 1, 1) * FACTOR)
            mixed = jnp.concatenate(mixed, axis=0).astype(BF16)
            attended = dot(wout_t_ref[...], mixed, 1, 0).astype(BF16)
            outer[...] += dot(mixed, ct, 1, 1)
            g_triple = jnp.concatenate(g_q + g_k + g_v, axis=0).astype(BF16)
            grads[:, : 3 * C] += dot(normed, g_triple, 1, 1)
            wide = dot(win_ref[...], g_triple, 1, 0).astype(BF16).astype(F32)
            block = (xt + attended.astype(F32)).astype(BF16)
            gain_acc[...] += wide * part
            scaled = wide * gain
            grad_part = inverse * (
                scaled
                - jnp.mean(scaled, axis=0, keepdims=True)
                - part * jnp.mean(scaled * part, axis=0, keepdims=True)
            )
            in_grad = (ct32 + grad_part).astype(BF16)
            out_w = out_w + dot(pick, block, 1, 1)
            ig_w = ig_w + dot(pick, in_grad, 1, 1)
        ext[0, :, span] = out_w.reshape(2, 6, 32, C)
        ext[1, :, span] = ig_w.reshape(2, 6, 32, C)
        return carry

    lax.fori_loop(0, TAB, row, 0)
    for k, ref in enumerate((out_ref, ig_ref)):
        ext[k, :, 0:3] = jnp.zeros((2, 3, 32, C), F32)
        ref[...] = ext[k, :, 0:18, 0:24, :].astype(BF16)
        lon_out[k] = ext[k, :, 0:18, 24:32, :].astype(BF16)
        lat_out[k] = ext[k, :, 18:21, 0:24, :].astype(BF16)
        cor_out[k] = ext[k, :, 18:21, 24:32, :].astype(BF16)

    blocks[...] = jnp.zeros_like(blocks)
    total = jnp.zeros((TAB * HEADS * 16, 384), F32)
    for c in range(WLON):
        for th in range(TAB * HEADS):
            blocks[th * 16 : th * 16 + AB, :] = dbias[th, c * AB : (c + 1) * AB, :]
        total = total + dot(blocks[...].astype(BF16), toeplitz(c), 1, 1)
    flat_t[...] = jnp.zeros_like(flat_t)
    for t in range(TAB):
        rows[...] = dot(heads_first(), total[t * 96 : (t + 1) * 96].astype(BF16), 0, 0)
        for ab_p, ab_r, start in segments():
            flat_t[t * 8 : t * 8 + 8, start : start + SPAN] = rows[
                ab_r * 8 : ab_r * 8 + 8, ab_p * SPAN : (ab_p + 1) * SPAN
            ]
    flat[...] = jnp.zeros_like(flat)
    for block in range(LANE_BLOCKS):
        for t in range(TAB):
            at = (block * TAB + t) * HEADS
            flat[at : at + HEADS, :] = flat_t[t * 8 : t * 8 + HEADS, block * 128 : (block + 1) * 128]

    chunks[...] = jnp.zeros_like(chunks)
    grads[:, 3 * C :] = outer[...]
    tile = 0
    for group in range(C // 8):
        for block in range(C * 4 // 128):
            chunk, slot = divmod(tile, G_ROWS // 8)
            chunks[chunk // 16, chunk % 16, slot * 8 : slot * 8 + 8, :] = grads[
                group * 8 : group * 8 + 8, block * 128 : (block + 1) * 128
            ]
            tile += 1
    for chunk in range(32):
        chunks[chunk // 16, chunk % 16, G_ROWS : G_ROWS + T_ROWS, :] = flat[chunk * T_ROWS : (chunk + 1) * T_ROWS]
    rest = gain_acc[...]
    gain_row = jnp.zeros((8, C), F32)
    for _ in range(3):
        low = rest.astype(BF16)
        rest = rest - low.astype(F32)
        gain_row = gain_row + dot(jnp.ones((8, POINTS), BF16), low, 1, 1)
    chunks[1, 13, 0:1, :] = gain_row[0:1, 0:128]
    chunks[1, 13, 1:2, 0:64] = gain_row[0:1, 128:192]
    me = ens_ref[0]
    keep_ref[...] = chunks[me]
    send_ref[...] = chunks[1 - me].astype(BF16)


def over_ens_kernel(keep_ref, got_ref, out_ref):
    out_ref[...] = (keep_ref[...] + got_ref[...].astype(F32)).astype(BF16)


def over_lon_kernel(got_ref, out_ref):
    total = jnp.sum(got_ref[...].astype(F32), axis=0).astype(BF16)
    for k in range(out_ref.shape[0]):
        out_ref[k] = total


def over_lat_kernel(got_ref, out_ref):
    got = got_ref[...].astype(F32)
    total = jnp.sum(got[:, : G_ROWS + 8], axis=0)
    shard = jnp.concatenate([total] + [got[k, G_ROWS : G_ROWS + T_ROWS] for k in range(8)], axis=0).astype(BF16)
    for k in range(out_ref.shape[0]):
        out_ref[k] = shard


def place_kernel(out_ref, grad_ref, lon_ref, lat_ref, cor_ref, out_whole, grad_whole):
    for k, (ref, whole) in enumerate(((out_ref, out_whole), (grad_ref, grad_whole))):
        left = ref[:, :, 0:8, :].astype(F32) + lon_ref[k].astype(F32)
        whole[:, 3:, 0:8, :] = left[:, 3:].astype(BF16)
        whole[:, 3:, 8:24, :] = ref[:, 3:, 8:24, :]
        top = lat_ref[k].astype(F32)
        corner = top[:, :, 0:8, :] + left[:, 0:3] + cor_ref[k].astype(F32)
        whole[:, 0:3, 0:8, :] = corner.astype(BF16)
        whole[:, 0:3, 8:24, :] = top[:, :, 8:24, :].astype(BF16)


def final_kernel(ens_ref, mine_ref, other_ref, in_ref, outer_ref, gain_ref, table_ref, both, tables, grads, full):
    me = ens_ref[0]
    both[me] = mine_ref[...].astype(F32)
    both[1 - me] = other_ref[...].astype(F32)
    tile = 0
    for group in range(C // 8):
        for block in range(C * 4 // 128):
            chunk, slot = divmod(tile, G_ROWS // 8)
            grads[group * 8 : group * 8 + 8, block * 128 : (block + 1) * 128] = both[
                chunk // 16, chunk % 16, slot * 8 : slot * 8 + 8, :
            ]
            tile += 1
    in_ref[...] = grads[:, 0 : 3 * C]
    outer_ref[...] = grads[:, 3 * C :]
    gain_ref[0:1, 0:128] = both[1, 13, 0:1, :]
    gain_ref[0:1, 128:192] = both[1, 13, 1:2, 0:64]
    for lat in range(8):
        for chunk in range(32):
            tables[lat, chunk * T_ROWS : (chunk + 1) * T_ROWS, :] = both[
                chunk // 16, chunk % 16, G_ROWS + 8 + lat * T_ROWS : G_ROWS + 8 + (lat + 1) * T_ROWS, :
            ]
    count = TAB * HEADS
    for lat in range(8):
        for block in range(LANE_BLOCKS):
            full[lat * count : (lat + 1) * count, block * 128 : (block + 1) * 128] = tables[
                lat, block * count : (block + 1) * count, :
            ]
    m = iota((144, 144), 0)
    h24 = (m * 43691) >> 20
    order = (iota((144, 144), 1) == (m - h24 * 24) * HEADS + h24).astype(BF16)
    ordered = dot(order, full[...].astype(BF16), 1, 0)
    for h in range(HEADS):
        table_ref[h] = ordered[h * 24 : (h + 1) * 24, :ENTRIES]


SMEM = pl.BlockSpec(memory_space=pltpu.SMEM)
WHOLE = pl.BlockSpec(memory_space=pltpu.VMEM)


def call(kernel, outs, args, scratch=()):
    specs = [SMEM if a.dtype == I32 and a.ndim == 1 else WHOLE for a in args]
    shapes = tuple(pltpu.VMEM(*o) if len(o) == 2 else jax.ShapeDtypeStruct(*o[:2]) for o in outs)
    return pl.pallas_call(
        kernel,
        out_shape=shapes,
        in_specs=specs,
        out_specs=tuple(WHOLE for _ in outs),
        scratch_shapes=[pltpu.VMEM(*x) for x in scratch],
        compiler_params=pltpu.CompilerParams(vmem_limit_bytes=56 * 2**20),
    )(*args)


def near(x):
    return pltpu.with_memory_space_constraint(x, pltpu.VMEM)


def passed(x, axes, sizes, moves):
    total = [()]
    for size in sizes:
        total = [t + (i,) for t in total for i in range(size)]

    def number(index):
        n = 0
        for i, size in zip(index, sizes):
            n = n * size + i % size
        return n

    pairs = [(number(t), number(tuple(i + m for i, m in zip(t, moves)))) for t in total]
    return lax.ppermute(x, axes, pairs)


def halo(lon_strip, lat_strip, corner, by):
    n_lon, n_lat = lax.axis_size("lon"), lax.axis_size("lat")
    return (
        passed(lon_strip, "lon", (n_lon,), (by,)),
        passed(lat_strip, "lat", (n_lat,), (by,)),
        passed(corner, ("lon", "lat"), (n_lon, n_lat), (by, by)),
    )


def local(inputs, cotangent, mask_ids, norm_gain, project_in, project_out, bias_table):
    x, y = inputs[0], cotangent[0]
    lat = lax.axis_index("lat").astype(I32).reshape(1)
    me = lax.axis_index("ens").astype(I32).reshape(1)
    strip_shapes = [((2, 2, 18, 8, C), BF16), ((2, 2, 3, 24, C), BF16), ((2, 2, 3, 8, C), BF16)]
    strips = halo(*call(strips_kernel, strip_shapes, (x, y)), -1)
    bias, win_t, wout_t, gain, regions = call(
        shadow_kernel,
        [
            ((TAB * HEADS, POINTS, POINTS), F32),
            ((3 * C, C), BF16),
            ((C, C), BF16),
            ((C, POINTS), F32),
            ((TAB, 2, 1, POINTS), F32),
        ],
        (
            lat, bias_table.transpose(1, 0, 2), norm_gain.reshape(1, C), project_in, project_out,
            mask_ids.transpose(1, 0, 2),
        ),
        [((TAB, HEADS, ENTRIES), F32), ((TAB, 96, 384), F32), ((TAB, 16, 128), F32)],
    )
    out, in_grad, lon_s, lat_s, cor_s, keep, send = call(
        main_kernel,
        [((2, 18, 24, C), BF16)] * 2 + strip_shapes + [((16, CHUNK, 128), F32), ((16, CHUNK, 128), BF16)],
        (
            me, x, y, *map(near, strips), near(regions), near(gain), project_in, near(win_t), project_out,
            near(wout_t), near(bias),
        ),
        [
            ((2, 2, 21, 32, C), F32),
            ((C, 4 * C), F32),
            ((C, C), F32),
            ((C, POINTS), F32),
            ((TAB * HEADS, POINTS, POINTS), F32),
            ((TAB * HEADS * 16, POINTS), F32),
            ((96, 384), F32),
            ((TAB * 8, LANE_BLOCKS * 128), F32),
            ((32 * T_ROWS, 128), F32),
            ((2, 16, CHUNK, 128), F32),
        ],
    )

    got = passed(send, "ens", (2,), (1,))
    strips = halo(lon_s, lat_s, cor_s, 1)
    (part,) = call(over_ens_kernel, [((16, CHUNK, 128), BF16)], (near(keep), near(got)))
    part = lax.all_to_all(part, "lon", 0, 0, tiled=True)
    part, *strips = lax.optimization_barrier((part, *strips))
    (part,) = call(over_lon_kernel, [((8, CHUNK, 128), BF16)], (near(part),))
    part = lax.all_to_all(part, "lat", 0, 0, tiled=True)
    (part,) = call(over_lat_kernel, [((16, SHARD, 128), BF16)], (near(part),))
    mine = lax.all_to_all(part, "lon", 0, 0, tiled=True)
    other = passed(mine, "ens", (2,), (1,))
    in_total, out_total, gain_total, table_total = call(
        final_kernel,
        [
            ((C, 3 * C), F32, None),
            ((C, C), F32, None),
            ((1, C), F32, None),
            ((HEADS, 24, ENTRIES), F32, None),
        ],
        (me, near(mine), near(other)),
        [
            ((2, 16, SHARD, 128), F32),
            ((8, 32 * T_ROWS, 128), F32),
            ((C, 4 * C), F32),
            ((144, LANE_BLOCKS * 128), F32),
        ],
    )
    out, in_grad = call(
        place_kernel,
        [((2, 18, 24, C), BF16, None)] * 2,
        (near(out), near(in_grad), *map(near, strips)),
    )
    return (
        out[None],
        in_grad[None],
        in_total,
        out_total,
        gain_total.reshape(C),
        table_total.transpose(1, 0, 2),
    )


def solution(mesh):
    return jax.shard_map(
        local,
        mesh=mesh,
        in_specs=(
            P("ens", None, "lat", "lon", None),
            P("ens", None, "lat", "lon", None),
            P(None, "lat", "lon"),
            P(),
            P(),
            P(),
            P(),
        ),
        out_specs=(
            P("ens", None, "lat", "lon", None),
            P("ens", None, "lat", "lon", None),
            P(),
            P(),
            P(),
            P(),
        ),
        check_vma=False,
    )
```

```python
import jax
import jax.numpy as jnp
from jax import lax
from jax.experimental import pallas as pl
from jax.experimental.pallas import tpu as pltpu
from jax.sharding import PartitionSpec as P

WL, WLAT, WLON = 2, 6, 12
AB = WL * WLAT
POINTS = AB * WLON
SPAN = 2 * WLON - 1
EPS = 1e-05
F32, BF16, I32 = jnp.float32, jnp.bfloat16, jnp.int32
C, HEADS, HD = 192, 6, 32
FACTOR = HD ** (-0.5)
TAB = 3
ENTRIES = AB * AB * SPAN
LANE_BLOCKS = -(-ENTRIES // 128)
CHUNK = 64
G_ROWS = 40
T_ROWS = 16
SHARD = 168


def dot(a, b, ca, cb):
    return lax.dot_general(a, b, (((ca,), (cb,)), ((), ())), preferred_element_type=F32)


def iota(shape, dim):
    return lax.broadcasted_iota(I32, shape, dim)


def segments():
    for ab_p in range(AB):
        a_p, b_p = divmod(ab_p, WLAT)
        for ab_r in range(AB):
            a_r, b_r = divmod(ab_r, WLAT)
            yield ab_p, ab_r, (((a_p * WL + a_r) * WLAT + b_p) * WLAT + b_r) * SPAN


def tokens():
    p = iota((1, POINTS), 1)
    c_p = (p * 21846) >> 18
    return c_p, p - c_p * AB


def toeplitz(c):
    c_p, ab_p = tokens()
    return (iota((384, POINTS), 0) == ab_p * SPAN + c_p + (WLON - 1 - c)).astype(BF16)


def heads_first():
    n = iota((96, 96), 0)
    return ((iota((96, 96), 1) == (n & 15) * 8 + (n >> 4)) & ((n & 15) < AB)).astype(BF16)


def strips_kernel(x_ref, y_ref, lon_ref, lat_ref, cor_ref):
    for k, ref in enumerate((x_ref, y_ref)):
        lon_ref[k] = ref[:, :, 0:8, :]
        lat_ref[k] = ref[:, 0:3, :, :]
        cor_ref[k] = ref[:, 0:3, 0:8, :]


def shadow_kernel(
    lat_ref, table_ref, gain_ref, win_ref, wout_ref, mask_ref,
    bias_ref, win_t_ref, wout_t_ref, gain_out, region_ref, own_ref, rows_ref, ids_ref,
):
    first = lat_ref[0] * TAB
    for t in range(TAB):
        for h in range(HEADS):
            own_ref[t, h : h + 1, :] = table_ref[h, pl.ds(first + t, 1), :]
    rows_ref[...] = jnp.zeros_like(rows_ref)
    for t in range(TAB):
        for ab_p, ab_r, start in segments():
            rows_ref[t, ab_r * 8 : ab_r * 8 + HEADS, ab_p * SPAN : (ab_p + 1) * SPAN] = own_ref[
                t, :, start : start + SPAN
            ]
    order = heads_first()
    pieces = []
    rest = [rows_ref[t] for t in range(TAB)]
    for _ in range(3):
        low = [r.astype(BF16) for r in rest]
        rest = [r - p.astype(F32) for r, p in zip(rest, low)]
        pieces.append(jnp.concatenate([dot(order, p, 1, 0).astype(BF16) for p in low], axis=0))
    for c in range(WLON):
        pick = toeplitz(c)
        full = dot(pieces[0], pick, 1, 0) + (dot(pieces[1], pick, 1, 0) + dot(pieces[2], pick, 1, 0))
        for th in range(TAB * HEADS):
            bias_ref[th, c * AB : (c + 1) * AB, :] = full[th * 16 : th * 16 + AB, :]
    win_t_ref[...] = win_ref[...].T
    wout_t_ref[...] = wout_ref[...].T
    column = jnp.broadcast_to(gain_ref[...], (8, C)).T
    gain_out[...] = jnp.broadcast_to(column[:, 0:1], (C, POINTS))
    ids_ref[...] = jnp.zeros_like(ids_ref)
    c_p, ab_p = tokens()
    for v in range(TAB):
        for b in range(WLAT):
            for a in range(WL):
                at = a * WLAT + b
                ids_ref[v, at : at + 1, 0:24] = mask_ref[v * WLAT + b, a : a + 1, :].astype(F32)
        for w in range(2):
            pick = (iota((128, POINTS), 0) == c_p + WLON * w).astype(BF16)
            spread = dot(ids_ref[v].astype(BF16), pick, 1, 0)
            own = jnp.where(iota((16, POINTS), 0) == ab_p, spread, 0.0)
            region_ref[v, w] = jnp.sum(own, axis=0, keepdims=True)


def main_kernel(
    ens_ref, x_ref, y_ref, lon_ref, lat_ref, cor_ref, region_ref, gain_ref, win_ref, win_t_ref, wout_ref,
    wout_t_ref, bias_ref,
    out_ref, ig_ref, lon_out, lat_out, keep_ref, send_ref,
    ext, grads, outer, gain_acc, dbias, blocks, rows, flat_t, flat, chunks,
):
    for k, ref in enumerate((x_ref, y_ref)):
        ext[k, :, 0:18, 0:24, :] = ref[...].astype(F32)
        ext[k, :, 0:18, 24:32, :] = lon_ref[k].astype(F32)
        ext[k, :, 18:21, 0:24, :] = lat_ref[k].astype(F32)
        ext[k, :, 18:21, 24:32, :] = cor_ref[k].astype(F32)
    grads[...] = jnp.zeros_like(grads)
    outer[...] = jnp.zeros_like(outer)
    gain_acc[...] = jnp.zeros_like(gain_acc)
    gain = gain_ref[...]
    heads = [(iota((POINTS, C), 1) >> 5) == h for h in range(HEADS)]
    c_p, ab_p = tokens()
    level = jnp.where(ab_p >= WLAT, 1, 0)
    place = (1 - level) * (WLAT * 32) + (ab_p - level * WLAT) * 32 + WLON // 2 + c_p

    def window(v, w, x_rows, y_rows):
        pick = (iota((384, POINTS), 0) == place + WLON * w).astype(BF16)
        xt = dot(x_rows, pick, 1, 0)
        ct32 = dot(y_rows, pick, 1, 0)
        yield
        ct = ct32.astype(BF16)
        center = xt - jnp.mean(xt, axis=0, keepdims=True)
        inverse = lax.rsqrt(jnp.mean(center * center, axis=0, keepdims=True) + EPS)
        part = center * inverse
        normed = (part * gain).astype(BF16)
        yield
        triple = dot(win_t_ref[...], normed, 1, 0).astype(BF16)
        grad_mixed = dot(wout_ref[...], ct, 1, 0).astype(BF16)
        yield
        natural = dot(normed, win_ref[...], 0, 0).astype(BF16)
        gm_n = dot(ct, wout_t_ref[...], 0, 0).astype(BF16)
        ids = region_ref[v, w]
        member = (iota((8, POINTS), 0).astype(F32) == ids).astype(BF16)
        barred = (dot(member, member, 0, 0) - 1.0) * 1e30
        yield
        q_n, k_n, v_n = natural[:, :C], natural[:, C : 2 * C], natural[:, 2 * C :]
        zero = jnp.zeros_like(k_n)
        k_heads = jnp.concatenate([jnp.where(m, k_n, zero) for m in heads], axis=0)
        v_heads = jnp.concatenate([jnp.where(m, v_n, zero) for m in heads], axis=0)
        all_scores = dot(k_heads, triple[:C], 1, 0)
        all_g_prob = dot(v_heads, grad_mixed, 1, 0)
        yield
        mixed, g_q, lows, g_lows = [], [], [], []
        for h in range(HEADS):
            lo, hi = h * HD, (h + 1) * HD
            part_h = slice(h * POINTS, (h + 1) * POINTS)
            scores = all_scores[part_h] * FACTOR + (bias_ref[v * HEADS + h] + barred)
            raised = jnp.exp(scores - jnp.max(scores, axis=0, keepdims=True))
            prob = raised * (1.0 / jnp.sum(raised, axis=0, keepdims=True))
            low = prob.astype(BF16)
            mixed.append(dot(triple[2 * C + lo : 2 * C + hi], low, 1, 0))
            g_prob = all_g_prob[part_h]
            g_score = prob * (g_prob - jnp.sum(prob * g_prob, axis=0, keepdims=True))
            if w == 0:
                dbias[v * HEADS + h] = g_score
            else:
                dbias[v * HEADS + h] += g_score
            g_low = g_score.astype(BF16)
            g_q.append(dot(triple[C + lo : C + hi], g_low, 1, 0) * FACTOR)
            lows.append(low)
            g_lows.append(g_low)
            yield
        all_g_v = dot(jnp.concatenate(lows, axis=0), gm_n, 1, 0)
        all_g_k = dot(jnp.concatenate(g_lows, axis=0), q_n, 1, 0)
        mixed = jnp.concatenate(mixed, axis=0).astype(BF16)
        attended = dot(wout_t_ref[...], mixed, 1, 0).astype(BF16)
        outer[...] += dot(mixed, ct, 1, 1)
        yield
        g_v, g_k = all_g_v[:POINTS], all_g_k[:POINTS]
        for h in range(1, HEADS):
            part_h = slice(h * POINTS, (h + 1) * POINTS)
            g_v = jnp.where(heads[h], all_g_v[part_h], g_v)
            g_k = jnp.where(heads[h], all_g_k[part_h], g_k)
        g_q = jnp.concatenate(g_q, axis=0).astype(BF16)
        g_k = (g_k * FACTOR).astype(BF16)
        g_v = g_v.astype(BF16)
        wide = dot(win_ref[:, :C], g_q, 1, 0)
        wide = wide + dot(win_ref[:, C : 2 * C], g_k, 1, 1) + dot(win_ref[:, 2 * C :], g_v, 1, 1)
        wide = wide.astype(BF16).astype(F32)
        yield
        grads[:, :C] += dot(normed, g_q, 1, 1)
        grads[:, C : 2 * C] += dot(normed, g_k, 1, 0)
        grads[:, 2 * C : 3 * C] += dot(normed, g_v, 1, 0)
        block = (xt + attended.astype(F32)).astype(BF16)
        gain_acc[...] += wide * part
        scaled = wide * gain
        grad_part = inverse * (
            scaled
            - jnp.mean(scaled, axis=0, keepdims=True)
            - part * jnp.mean(scaled * part, axis=0, keepdims=True)
        )
        in_grad = (ct32 + grad_part).astype(BF16)
        yield
        yield dot(pick, block, 1, 1), dot(pick, in_grad, 1, 1)

    def rows_of(k, v):
        return ext[k, :, 6 * v + 3 : 6 * v + 9].reshape(384, C).astype(BF16).T

    def group(chosen):
        results = [None]
        todo = [window(v, w, rows_of(0, v), rows_of(1, v)) for v in chosen for w in range(2)]
        while results[0] is None:
            results = [next(g) for g in todo]
        for i, v in enumerate(chosen):
            for k in range(2):
                total = results[2 * i][k] + results[2 * i + 1][k]
                ext[k, :, 6 * v + 3 : 6 * v + 9] = total.reshape(2, 6, 32, C)

    group(range(TAB))
    for k, ref in enumerate((out_ref, ig_ref)):
        ext[k, :, 0:3] = jnp.zeros((2, 3, 32, C), F32)
        ref[...] = ext[k, :, 0:18, 0:24, :].astype(BF16)
        lon_out[k] = ext[k, :, 3:21, 24:32, :].astype(BF16)
        lat_out[k] = ext[k, :, 18:21, 0:24, :].astype(BF16)

    blocks[...] = jnp.zeros_like(blocks)
    total = jnp.zeros((TAB * HEADS * 16, 384), F32)
    for c in range(WLON):
        for th in range(TAB * HEADS):
            blocks[th * 16 : th * 16 + AB, :] = dbias[th, c * AB : (c + 1) * AB, :]
        total = total + dot(blocks[...].astype(BF16), toeplitz(c), 1, 1)
    flat_t[...] = jnp.zeros_like(flat_t)
    for t in range(TAB):
        rows[...] = dot(heads_first(), total[t * 96 : (t + 1) * 96].astype(BF16), 0, 0)
        for ab_p, ab_r, start in segments():
            flat_t[t * 8 : t * 8 + 8, start : start + SPAN] = rows[
                ab_r * 8 : ab_r * 8 + 8, ab_p * SPAN : (ab_p + 1) * SPAN
            ]
    flat[...] = jnp.zeros_like(flat)
    for block in range(LANE_BLOCKS):
        for t in range(TAB):
            at = (block * TAB + t) * HEADS
            flat[at : at + HEADS, :] = flat_t[t * 8 : t * 8 + HEADS, block * 128 : (block + 1) * 128]

    chunks[...] = jnp.zeros_like(chunks)
    grads[:, 3 * C :] = outer[...]
    tile = 0
    for group in range(C // 8):
        for block in range(C * 4 // 128):
            chunk, slot = divmod(tile, G_ROWS // 8)
            chunks[chunk // 16, chunk % 16, slot * 8 : slot * 8 + 8, :] = grads[
                group * 8 : group * 8 + 8, block * 128 : (block + 1) * 128
            ]
            tile += 1
    for chunk in range(32):
        chunks[chunk // 16, chunk % 16, G_ROWS : G_ROWS + T_ROWS, :] = flat[chunk * T_ROWS : (chunk + 1) * T_ROWS]
    rest = gain_acc[...]
    gain_row = jnp.zeros((8, C), F32)
    for _ in range(3):
        low = rest.astype(BF16)
        rest = rest - low.astype(F32)
        gain_row = gain_row + dot(jnp.ones((8, POINTS), BF16), low, 1, 1)
    chunks[1, 13, 0:1, :] = gain_row[0:1, 0:128]
    chunks[1, 13, 1:2, 0:64] = gain_row[0:1, 128:192]
    me = ens_ref[0]
    keep_ref[...] = chunks[me]
    send_ref[...] = chunks[1 - me].astype(BF16)


def over_ens_kernel(keep_ref, got_ref, out_ref):
    out_ref[...] = (keep_ref[...] + got_ref[...].astype(F32)).astype(BF16)


def over_lon_kernel(got_ref, out_ref):
    total = jnp.sum(got_ref[...].astype(F32), axis=0).astype(BF16)
    for k in range(out_ref.shape[0]):
        out_ref[k] = total


def over_lat_kernel(got_ref, lon_ref, lat_ref, out_ref, lat_out):
    lat_out[:, :, :, 8:24, :] = lat_ref[:, :, :, 8:24, :]
    corner = lat_ref[:, :, :, 0:8, :].astype(F32) + lon_ref[:, :, 15:18].astype(F32)
    lat_out[:, :, :, 0:8, :] = corner.astype(BF16)
    got = got_ref[...].astype(F32)
    total = jnp.sum(got[:, :G_ROWS], axis=0)
    shard = jnp.concatenate([total] + [got[k, G_ROWS : G_ROWS + T_ROWS] for k in range(8)], axis=0).astype(BF16)
    for k in range(out_ref.shape[0]):
        out_ref[k] = shard


def place_kernel(out_ref, grad_ref, lon_ref, lat_ref, out_whole, grad_whole):
    for k, (ref, whole) in enumerate(((out_ref, out_whole), (grad_ref, grad_whole))):
        left = ref[:, 3:, 0:8, :].astype(F32) + lon_ref[k, :, 0:15].astype(F32)
        whole[:, 3:, 0:8, :] = left.astype(BF16)
        whole[:, 3:, 8:24, :] = ref[:, 3:, 8:24, :]
        whole[:, 0:3] = lat_ref[k]


def final_kernel(ens_ref, mine_ref, other_ref, in_ref, outer_ref, gain_ref, table_ref, both, tables, grads, full):
    me = ens_ref[0]
    both[me] = mine_ref[...].astype(F32)
    both[1 - me] = other_ref[...].astype(F32)
    tile = 0
    for group in range(C // 8):
        for block in range(C * 4 // 128):
            chunk, slot = divmod(tile, G_ROWS // 8)
            grads[group * 8 : group * 8 + 8, block * 128 : (block + 1) * 128] = both[
                chunk // 16, chunk % 16, slot * 8 : slot * 8 + 8, :
            ]
            tile += 1
    in_ref[...] = grads[:, 0 : 3 * C]
    outer_ref[...] = grads[:, 3 * C :]
    gain_ref[0:1, 0:128] = both[1, 13, 0:1, :]
    gain_ref[0:1, 128:192] = both[1, 13, 1:2, 0:64]
    for lat in range(8):
        for chunk in range(32):
            tables[lat, chunk * T_ROWS : (chunk + 1) * T_ROWS, :] = both[
                chunk // 16, chunk % 16, G_ROWS + lat * T_ROWS : G_ROWS + (lat + 1) * T_ROWS, :
            ]
    count = TAB * HEADS
    for lat in range(8):
        for block in range(LANE_BLOCKS):
            full[lat * count : (lat + 1) * count, block * 128 : (block + 1) * 128] = tables[
                lat, block * count : (block + 1) * count, :
            ]
    m = iota((144, 144), 0)
    h24 = (m * 43691) >> 20
    order = (iota((144, 144), 1) == (m - h24 * 24) * HEADS + h24).astype(BF16)
    ordered = dot(order, full[...].astype(BF16), 1, 0)
    for h in range(HEADS):
        table_ref[h] = ordered[h * 24 : (h + 1) * 24, :ENTRIES]


SMEM = pl.BlockSpec(memory_space=pltpu.SMEM)
WHOLE = pl.BlockSpec(memory_space=pltpu.VMEM)


def call(kernel, outs, args, scratch=()):
    specs = [SMEM if a.dtype == I32 and a.ndim == 1 else WHOLE for a in args]
    shapes = tuple(pltpu.VMEM(*o) if len(o) == 2 else jax.ShapeDtypeStruct(*o[:2]) for o in outs)
    return pl.pallas_call(
        kernel,
        out_shape=shapes,
        in_specs=specs,
        out_specs=tuple(WHOLE for _ in outs),
        scratch_shapes=[pltpu.VMEM(*x) for x in scratch],
        compiler_params=pltpu.CompilerParams(vmem_limit_bytes=56 * 2**20),
    )(*args)


def near(x):
    return pltpu.with_memory_space_constraint(x, pltpu.VMEM)


def passed(x, axes, sizes, moves):
    total = [()]
    for size in sizes:
        total = [t + (i,) for t in total for i in range(size)]

    def number(index):
        n = 0
        for i, size in zip(index, sizes):
            n = n * size + i % size
        return n

    pairs = [(number(t), number(tuple(i + m for i, m in zip(t, moves)))) for t in total]
    return lax.ppermute(x, axes, pairs)


def halo(lon_strip, lat_strip, corner, by):
    n_lon, n_lat = lax.axis_size("lon"), lax.axis_size("lat")
    return (
        passed(lon_strip, "lon", (n_lon,), (by,)),
        passed(lat_strip, "lat", (n_lat,), (by,)),
        passed(corner, ("lon", "lat"), (n_lon, n_lat), (by, by)),
    )


STRIPS = [((2, 2, 18, 8, C), BF16), ((2, 2, 3, 24, C), BF16), ((2, 2, 3, 8, C), BF16)]


def run_shadow(lat, bias_table, norm_gain, project_in, project_out, mask_ids):
    return call(
        shadow_kernel,
        [
            ((TAB * HEADS, POINTS, POINTS), F32),
            ((3 * C, C), BF16),
            ((C, C), BF16),
            ((C, POINTS), F32),
            ((TAB, 2, 1, POINTS), F32),
        ],
        (
            lat, bias_table.transpose(1, 0, 2), norm_gain.reshape(1, C), project_in, project_out,
            mask_ids.transpose(1, 0, 2),
        ),
        [((TAB, HEADS, ENTRIES), F32), ((TAB, 96, 384), F32), ((TAB, 16, 128), F32)],
    )


def run_main(me, x, y, strips, regions, gain, project_in, win_t, project_out, wout_t, bias):
    return call(
        main_kernel,
        [((2, 18, 24, C), BF16)] * 2 + STRIPS[:2] + [((16, CHUNK, 128), F32), ((16, CHUNK, 128), BF16)],
        (
            me, x, y, *map(near, strips), near(regions), near(gain), project_in, near(win_t), project_out,
            near(wout_t), near(bias),
        ),
        [
            ((2, 2, 21, 32, C), F32),
            ((C, 4 * C), F32),
            ((C, C), F32),
            ((C, POINTS), F32),
            ((TAB * HEADS, POINTS, POINTS), F32),
            ((TAB * HEADS * 16, POINTS), F32),
            ((96, 384), F32),
            ((TAB * 8, LANE_BLOCKS * 128), F32),
            ((32 * T_ROWS, 128), F32),
            ((2, 16, CHUNK, 128), F32),
        ],
    )


def local(inputs, cotangent, mask_ids, norm_gain, project_in, project_out, bias_table):
    x, y = inputs[0], cotangent[0]
    lat = lax.axis_index("lat").astype(I32).reshape(1)
    me = lax.axis_index("ens").astype(I32).reshape(1)
    strips = halo(*call(strips_kernel, STRIPS, (x, y)), -1)
    bias, win_t, wout_t, gain, regions = run_shadow(lat, bias_table, norm_gain, project_in, project_out, mask_ids)
    out, in_grad, lon_s, lat_s, keep, send = run_main(
        me, x, y, strips, regions, gain, project_in, win_t, project_out, wout_t, bias
    )
    got = passed(send, "ens", (2,), (1,))
    (part,) = call(over_ens_kernel, [((16, CHUNK, 128), BF16)], (near(keep), near(got)))
    part = lax.all_to_all(part, "lon", 0, 0, tiled=True)
    (part,) = call(over_lon_kernel, [((8, CHUNK, 128), BF16)], (near(part),))
    lon_s = passed(lon_s, "lon", (lax.axis_size("lon"),), (1,))
    part = lax.all_to_all(part, "lat", 0, 0, tiled=True)
    part, lat_s = call(
        over_lat_kernel,
        [((16, SHARD, 128), BF16), STRIPS[1]],
        (near(part), near(lon_s), near(lat_s)),
    )
    lat_s = passed(lat_s, "lat", (lax.axis_size("lat"),), (1,))
    mine = lax.all_to_all(part, "lon", 0, 0, tiled=True)
    mine, lat_s = lax.optimization_barrier((mine, lat_s))
    other = passed(mine, "ens", (2,), (1,))
    in_total, out_total, gain_total, table_total = call(
        final_kernel,
        [
            ((C, 3 * C), F32, None),
            ((C, C), F32, None),
            ((1, C), F32, None),
            ((HEADS, 24, ENTRIES), F32, None),
        ],
        (me, near(mine), near(other)),
        [
            ((2, 16, SHARD, 128), F32),
            ((8, 32 * T_ROWS, 128), F32),
            ((C, 4 * C), F32),
            ((144, LANE_BLOCKS * 128), F32),
        ],
    )
    out, in_grad = call(
        place_kernel,
        [((2, 18, 24, C), BF16, None)] * 2,
        (near(out), near(in_grad), near(lon_s), near(lat_s)),
    )
    return (
        out[None],
        in_grad[None],
        in_total,
        out_total,
        gain_total.reshape(C),
        table_total.transpose(1, 0, 2),
    )


def solution(mesh):
    return jax.shard_map(
        local,
        mesh=mesh,
        in_specs=(
            P("ens", None, "lat", "lon", None),
            P("ens", None, "lat", "lon", None),
            P(None, "lat", "lon"),
            P(),
            P(),
            P(),
            P(),
        ),
        out_specs=(
            P("ens", None, "lat", "lon", None),
            P("ens", None, "lat", "lon", None),
            P(),
            P(),
            P(),
            P(),
        ),
        check_vma=False,
    )
```

```python
import jax
import jax.numpy as jnp
from jax import lax
from jax.experimental import pallas as pl
from jax.experimental.pallas import tpu as pltpu
from jax.sharding import PartitionSpec as P

WL, WLAT, WLON = 2, 6, 12
AB = WL * WLAT
POINTS = AB * WLON
SPAN = 2 * WLON - 1
EPS = 1e-05
F32, BF16, I32 = jnp.float32, jnp.bfloat16, jnp.int32
C, HEADS, HD = 192, 6, 32
FACTOR = HD ** (-0.5)
TAB = 3
ENTRIES = AB * AB * SPAN
LANE_BLOCKS = -(-ENTRIES // 128)
CHUNK = 64
G_ROWS = 40
T_ROWS = 16
SHARD = 168


def dot(a, b, ca, cb):
    return lax.dot_general(a, b, (((ca,), (cb,)), ((), ())), preferred_element_type=F32)


def iota(shape, dim):
    return lax.broadcasted_iota(I32, shape, dim)


def segments():
    for ab_p in range(AB):
        a_p, b_p = divmod(ab_p, WLAT)
        for ab_r in range(AB):
            a_r, b_r = divmod(ab_r, WLAT)
            yield ab_p, ab_r, (((a_p * WL + a_r) * WLAT + b_p) * WLAT + b_r) * SPAN


def tokens():
    p = iota((1, POINTS), 1)
    c_p = (p * 21846) >> 18
    return c_p, p - c_p * AB


def toeplitz(c):
    c_p, ab_p = tokens()
    return (iota((384, POINTS), 0) == ab_p * SPAN + c_p + (WLON - 1 - c)).astype(BF16)


def heads_first():
    n = iota((96, 96), 0)
    return ((iota((96, 96), 1) == (n & 15) * 8 + (n >> 4)) & ((n & 15) < AB)).astype(BF16)


def strips_kernel(x_ref, y_ref, lon_ref, lat_ref, cor_ref):
    for k, ref in enumerate((x_ref, y_ref)):
        lon_ref[k] = ref[:, :, 0:8, :]
        lat_ref[k] = ref[:, 0:3, :, :]
        cor_ref[k] = ref[:, 0:3, 0:8, :]


def shadow_kernel(
    lat_ref, table_ref, gain_ref, win_ref, wout_ref, mask_ref,
    bias_ref, win_t_ref, wout_t_ref, gain_out, region_ref, own_ref, rows_ref, ids_ref,
):
    first = lat_ref[0] * TAB
    for t in range(TAB):
        for h in range(HEADS):
            own_ref[t, h : h + 1, :] = table_ref[h, pl.ds(first + t, 1), :]
    rows_ref[...] = jnp.zeros_like(rows_ref)
    for t in range(TAB):
        for ab_p, ab_r, start in segments():
            rows_ref[t, ab_r * 8 : ab_r * 8 + HEADS, ab_p * SPAN : (ab_p + 1) * SPAN] = own_ref[
                t, :, start : start + SPAN
            ]
    order = heads_first()
    m = iota((1, 384), 1)
    x = (m * 21846) >> 18
    swap = (iota((384, 384), 0) == (m - x * AB) * SPAN + x).astype(BF16)
    full = 0.0
    rest = [rows_ref[t] for t in range(TAB)]
    for _ in range(3):
        low = [r.astype(BF16) for r in rest]
        rest = [r - p.astype(F32) for r, p in zip(rest, low)]
        full = full + dot(jnp.concatenate([dot(order, p, 1, 0).astype(BF16) for p in low], axis=0), swap, 1, 0)
    for c in range(WLON):
        start = (WLON - 1 - c) * AB
        part = full[:, start : start + POINTS]
        for th in range(TAB * HEADS):
            bias_ref[th, c * AB : (c + 1) * AB, :] = part[th * 16 : th * 16 + AB, :]
    win_t_ref[...] = win_ref[...].T
    wout_t_ref[...] = wout_ref[...].T
    column = jnp.broadcast_to(gain_ref[...], (8, C)).T
    gain_out[...] = jnp.broadcast_to(column[:, 0:1], (C, POINTS))
    ids_ref[...] = jnp.zeros_like(ids_ref)
    c_p, ab_p = tokens()
    for v in range(TAB):
        for b in range(WLAT):
            for a in range(WL):
                at = a * WLAT + b
                ids_ref[v, at : at + 1, 0:24] = mask_ref[v * WLAT + b, a : a + 1, :].astype(F32)
        for w in range(2):
            pick = (iota((128, POINTS), 0) == c_p + WLON * w).astype(BF16)
            spread = dot(ids_ref[v].astype(BF16), pick, 1, 0)
            own = jnp.where(iota((16, POINTS), 0) == ab_p, spread, 0.0)
            region_ref[v, w] = jnp.sum(own, axis=0, keepdims=True)


def windows(weights, sums, save):
    region_ref, gain_ref, win_ref, win_t_ref, wout_ref, wout_t_ref, bias_ref = weights
    grads, outer, gain_acc = sums
    gain = gain_ref[...]
    heads = [(iota((POINTS, C), 1) >> 5) == h for h in range(HEADS)]
    c_p, ab_p = tokens()
    level = jnp.where(ab_p >= WLAT, 1, 0)
    place = (1 - level) * (WLAT * 32) + (ab_p - level * WLAT) * 32 + WLON // 2 + c_p

    def window(v, w, x_rows, y_rows):
        pick = (iota((384, POINTS), 0) == place + WLON * w).astype(BF16)
        xt = dot(x_rows, pick, 1, 0)
        ct32 = dot(y_rows, pick, 1, 0)
        yield
        ct = ct32.astype(BF16)
        center = xt - jnp.mean(xt, axis=0, keepdims=True)
        inverse = lax.rsqrt(jnp.mean(center * center, axis=0, keepdims=True) + EPS)
        part = center * inverse
        normed = (part * gain).astype(BF16)
        yield
        triple = dot(win_t_ref[...], normed, 1, 0).astype(BF16)
        grad_mixed = dot(wout_ref[...], ct, 1, 0).astype(BF16)
        yield
        natural = dot(normed, win_ref[...], 0, 0).astype(BF16)
        gm_n = dot(ct, wout_t_ref[...], 0, 0).astype(BF16)
        ids = region_ref[v, w]
        member = (iota((8, POINTS), 0).astype(F32) == ids).astype(BF16)
        barred = (dot(member, member, 0, 0) - 1.0) * 1e30
        yield
        q_n, k_n, v_n = natural[:, :C], natural[:, C : 2 * C], natural[:, 2 * C :]
        zero = jnp.zeros_like(k_n)
        k_heads = jnp.concatenate([jnp.where(m, k_n, zero) for m in heads], axis=0)
        v_heads = jnp.concatenate([jnp.where(m, v_n, zero) for m in heads], axis=0)
        all_scores = dot(k_heads, triple[:C], 1, 0)
        all_g_prob = dot(v_heads, grad_mixed, 1, 0)
        yield
        mixed, g_q, lows, g_lows = [], [], [], []
        for h in range(HEADS):
            lo, hi = h * HD, (h + 1) * HD
            part_h = slice(h * POINTS, (h + 1) * POINTS)
            scores = all_scores[part_h] * FACTOR + (bias_ref[v * HEADS + h] + barred)
            raised = jnp.exp(scores - jnp.max(scores, axis=0, keepdims=True))
            prob = raised * (1.0 / jnp.sum(raised, axis=0, keepdims=True))
            low = prob.astype(BF16)
            mixed.append(dot(triple[2 * C + lo : 2 * C + hi], low, 1, 0))
            g_prob = all_g_prob[part_h]
            g_score = prob * (g_prob - jnp.sum(prob * g_prob, axis=0, keepdims=True))
            save(v, w, h, g_score)
            g_low = g_score.astype(BF16)
            g_q.append(dot(triple[C + lo : C + hi], g_low, 1, 0) * FACTOR)
            lows.append(low)
            g_lows.append(g_low)
            yield
        all_g_v = dot(jnp.concatenate(lows, axis=0), gm_n, 1, 0)
        all_g_k = dot(jnp.concatenate(g_lows, axis=0), q_n, 1, 0)
        mixed = jnp.concatenate(mixed, axis=0).astype(BF16)
        attended = dot(wout_t_ref[...], mixed, 1, 0).astype(BF16)
        outer[...] += dot(mixed, ct, 1, 1)
        yield
        g_v, g_k = all_g_v[:POINTS], all_g_k[:POINTS]
        for h in range(1, HEADS):
            part_h = slice(h * POINTS, (h + 1) * POINTS)
            g_v = jnp.where(heads[h], all_g_v[part_h], g_v)
            g_k = jnp.where(heads[h], all_g_k[part_h], g_k)
        g_q = jnp.concatenate(g_q, axis=0).astype(BF16)
        g_k = (g_k * FACTOR).astype(BF16)
        g_v = g_v.astype(BF16)
        wide = dot(win_ref[:, :C], g_q, 1, 0)
        wide = wide + dot(win_ref[:, C : 2 * C], g_k, 1, 1) + dot(win_ref[:, 2 * C :], g_v, 1, 1)
        wide = wide.astype(BF16).astype(F32)
        yield
        grads[:, :C] += dot(normed, g_q, 1, 1)
        grads[:, C : 2 * C] += dot(normed, g_k, 1, 0)
        grads[:, 2 * C : 3 * C] += dot(normed, g_v, 1, 0)
        block = (xt + attended.astype(F32)).astype(BF16)
        gain_acc[...] += wide * part
        scaled = wide * gain
        grad_part = inverse * (
            scaled
            - jnp.mean(scaled, axis=0, keepdims=True)
            - part * jnp.mean(scaled * part, axis=0, keepdims=True)
        )
        in_grad = (ct32 + grad_part).astype(BF16)
        yield
        yield dot(pick, block, 1, 1), dot(pick, in_grad, 1, 1)

    return window


def interleaved(window, ext, chosen):
    def rows_of(k, v):
        return ext[k, :, 6 * v + 3 : 6 * v + 9].reshape(384, C).astype(BF16).T

    results = [None]
    todo = [window(v, w, rows_of(0, v), rows_of(1, v)) for v, w in chosen]
    while results[0] is None:
        results = [next(g) for g in todo]
    return dict(zip(chosen, results))


def inner_kernel(
    x_ref, y_ref, region_ref, gain_ref, win_ref, win_t_ref, wout_ref, wout_t_ref, bias_ref,
    rows_ref, grads, outer, gain_acc, dbias, ext,
):
    for k, ref in enumerate((x_ref, y_ref)):
        ext[k, :, :, 0:24, :] = ref[:, 0:15].astype(F32)
        ext[k, :, :, 24:32, :] = jnp.zeros((2, 15, 8, C), F32)
    for ref in (grads, outer, gain_acc):
        ref[...] = jnp.zeros_like(ref)

    def save(v, w, h, g_score):
        dbias[v * HEADS + h] = g_score

    weights = (region_ref, gain_ref, win_ref, win_t_ref, wout_ref, wout_t_ref, bias_ref)
    got = interleaved(windows(weights, (grads, outer, gain_acc), save), ext, [(0, 0), (1, 0)])
    for v in range(2):
        for k in range(2):
            rows_ref[k, v] = got[v, 0][k]


def main_kernel(
    ens_ref, x_ref, y_ref, lon_ref, lat_ref, cor_ref, region_ref, gain_ref, win_ref, win_t_ref, wout_ref,
    wout_t_ref, bias_ref, rows_in, grads_in, outer_in, gain_in, dbias_in,
    out_ref, ig_ref, lon_out, lat_out, keep_ref, send_ref,
    ext, grads, outer, gain_acc, dbias, blocks, rows, flat_t, flat, chunks,
):
    for k, ref in enumerate((x_ref, y_ref)):
        ext[k, :, 0:18, 0:24, :] = ref[...].astype(F32)
        ext[k, :, 0:18, 24:32, :] = lon_ref[k].astype(F32)
        ext[k, :, 18:21, 0:24, :] = lat_ref[k].astype(F32)
        ext[k, :, 18:21, 24:32, :] = cor_ref[k].astype(F32)
    grads[:, : 3 * C] = grads_in[...]
    outer[...] = outer_in[...]
    gain_acc[...] = gain_in[...]

    def save(v, w, h, g_score):
        at = v * HEADS + h
        if v < 2:
            dbias[at] = dbias_in[at] + g_score
        elif w == 0:
            dbias[at] = g_score
        else:
            dbias[at] += g_score

    weights = (region_ref, gain_ref, win_ref, win_t_ref, wout_ref, wout_t_ref, bias_ref)
    got = interleaved(
        windows(weights, (grads, outer, gain_acc), save), ext, [(0, 1), (1, 1), (2, 0), (2, 1)]
    )
    for v in range(TAB):
        for k in range(2):
            first = rows_in[k, v] if v < 2 else got[v, 0][k]
            ext[k, :, 6 * v + 3 : 6 * v + 9] = (first + got[v, 1][k]).reshape(2, 6, 32, C)
    for k, ref in enumerate((out_ref, ig_ref)):
        ext[k, :, 0:3] = jnp.zeros((2, 3, 32, C), F32)
        ref[...] = ext[k, :, 0:18, 0:24, :].astype(BF16)
        lon_out[k] = ext[k, :, 3:21, 24:32, :].astype(BF16)
        lat_out[k] = ext[k, :, 18:21, 0:24, :].astype(BF16)

    blocks[...] = jnp.zeros_like(blocks)
    total = jnp.zeros((TAB * HEADS * 16, 384), F32)
    for c in range(WLON):
        for th in range(TAB * HEADS):
            blocks[th * 16 : th * 16 + AB, :] = dbias[th, c * AB : (c + 1) * AB, :]
        total = total + dot(blocks[...].astype(BF16), toeplitz(c), 1, 1)
    flat_t[...] = jnp.zeros_like(flat_t)
    for t in range(TAB):
        rows[...] = dot(heads_first(), total[t * 96 : (t + 1) * 96].astype(BF16), 0, 0)
        for ab_p, ab_r, start in segments():
            flat_t[t * 8 : t * 8 + 8, start : start + SPAN] = rows[
                ab_r * 8 : ab_r * 8 + 8, ab_p * SPAN : (ab_p + 1) * SPAN
            ]
    flat[...] = jnp.zeros_like(flat)
    for block in range(LANE_BLOCKS):
        for t in range(TAB):
            at = (block * TAB + t) * HEADS
            flat[at : at + HEADS, :] = flat_t[t * 8 : t * 8 + HEADS, block * 128 : (block + 1) * 128]

    chunks[...] = jnp.zeros_like(chunks)
    grads[:, 3 * C :] = outer[...]
    tile = 0
    for group in range(C // 8):
        for block in range(C * 4 // 128):
            chunk, slot = divmod(tile, G_ROWS // 8)
            chunks[chunk // 16, chunk % 16, slot * 8 : slot * 8 + 8, :] = grads[
                group * 8 : group * 8 + 8, block * 128 : (block + 1) * 128
            ]
            tile += 1
    for chunk in range(32):
        chunks[chunk // 16, chunk % 16, G_ROWS : G_ROWS + T_ROWS, :] = flat[chunk * T_ROWS : (chunk + 1) * T_ROWS]
    rest = gain_acc[...]
    gain_row = jnp.zeros((8, C), F32)
    for _ in range(3):
        low = rest.astype(BF16)
        rest = rest - low.astype(F32)
        gain_row = gain_row + dot(jnp.ones((8, POINTS), BF16), low, 1, 1)
    chunks[1, 13, 0:1, :] = gain_row[0:1, 0:128]
    chunks[1, 13, 1:2, 0:64] = gain_row[0:1, 128:192]
    me = ens_ref[0]
    keep_ref[...] = chunks[me]
    send_ref[...] = chunks[1 - me].astype(BF16)


def over_ens_kernel(keep_ref, got_ref, out_ref):
    out_ref[...] = (keep_ref[...] + got_ref[...].astype(F32)).astype(BF16)


def over_lon_kernel(got_ref, out_ref):
    total = jnp.sum(got_ref[...].astype(F32), axis=0).astype(BF16)
    for k in range(out_ref.shape[0]):
        out_ref[k] = total


def over_lat_kernel(got_ref, lon_ref, lat_ref, out_ref, lat_out):
    lat_out[:, :, :, 8:24, :] = lat_ref[:, :, :, 8:24, :]
    corner = lat_ref[:, :, :, 0:8, :].astype(F32) + lon_ref[:, :, 15:18].astype(F32)
    lat_out[:, :, :, 0:8, :] = corner.astype(BF16)
    got = got_ref[...].astype(F32)
    total = jnp.sum(got[:, :G_ROWS], axis=0)
    shard = jnp.concatenate([total] + [got[k, G_ROWS : G_ROWS + T_ROWS] for k in range(8)], axis=0).astype(BF16)
    for k in range(out_ref.shape[0]):
        out_ref[k] = shard


def place_kernel(out_ref, grad_ref, lon_ref, lat_ref, out_whole, grad_whole):
    for k, (ref, whole) in enumerate(((out_ref, out_whole), (grad_ref, grad_whole))):
        left = ref[:, 3:, 0:8, :].astype(F32) + lon_ref[k, :, 0:15].astype(F32)
        whole[:, 3:, 0:8, :] = left.astype(BF16)
        whole[:, 3:, 8:24, :] = ref[:, 3:, 8:24, :]
        whole[:, 0:3] = lat_ref[k]


def final_kernel(ens_ref, mine_ref, other_ref, in_ref, outer_ref, gain_ref, table_ref, both, tables, grads, full):
    me = ens_ref[0]
    both[me] = mine_ref[...].astype(F32)
    both[1 - me] = other_ref[...].astype(F32)
    tile = 0
    for group in range(C // 8):
        for block in range(C * 4 // 128):
            chunk, slot = divmod(tile, G_ROWS // 8)
            grads[group * 8 : group * 8 + 8, block * 128 : (block + 1) * 128] = both[
                chunk // 16, chunk % 16, slot * 8 : slot * 8 + 8, :
            ]
            tile += 1
    in_ref[...] = grads[:, 0 : 3 * C]
    outer_ref[...] = grads[:, 3 * C :]
    gain_ref[0:1, 0:128] = both[1, 13, 0:1, :]
    gain_ref[0:1, 128:192] = both[1, 13, 1:2, 0:64]
    for lat in range(8):
        for chunk in range(32):
            tables[lat, chunk * T_ROWS : (chunk + 1) * T_ROWS, :] = both[
                chunk // 16, chunk % 16, G_ROWS + lat * T_ROWS : G_ROWS + (lat + 1) * T_ROWS, :
            ]
    count = TAB * HEADS
    for lat in range(8):
        for block in range(LANE_BLOCKS):
            full[lat * count : (lat + 1) * count, block * 128 : (block + 1) * 128] = tables[
                lat, block * count : (block + 1) * count, :
            ]
    m = iota((144, 144), 0)
    h24 = (m * 43691) >> 20
    order = (iota((144, 144), 1) == (m - h24 * 24) * HEADS + h24).astype(BF16)
    ordered = dot(order, full[...].astype(BF16), 1, 0)
    for h in range(HEADS):
        table_ref[h] = ordered[h * 24 : (h + 1) * 24, :ENTRIES]


SMEM = pl.BlockSpec(memory_space=pltpu.SMEM)
WHOLE = pl.BlockSpec(memory_space=pltpu.VMEM)


def call(kernel, outs, args, scratch=(), room=24):
    specs = [SMEM if a.dtype == I32 and a.ndim == 1 else WHOLE for a in args]
    shapes = tuple(pltpu.VMEM(*o) if len(o) == 2 else jax.ShapeDtypeStruct(*o[:2]) for o in outs)
    return pl.pallas_call(
        kernel,
        out_shape=shapes,
        in_specs=specs,
        out_specs=tuple(WHOLE for _ in outs),
        scratch_shapes=[pltpu.VMEM(*x) for x in scratch],
        compiler_params=pltpu.CompilerParams(vmem_limit_bytes=room * 2**20),
    )(*args)


def near(x):
    return pltpu.with_memory_space_constraint(x, pltpu.VMEM)


def passed(x, axes, sizes, moves):
    total = [()]
    for size in sizes:
        total = [t + (i,) for t in total for i in range(size)]

    def number(index):
        n = 0
        for i, size in zip(index, sizes):
            n = n * size + i % size
        return n

    pairs = [(number(t), number(tuple(i + m for i, m in zip(t, moves)))) for t in total]
    return lax.ppermute(x, axes, pairs)


def halo(lon_strip, lat_strip, corner, by):
    n_lon, n_lat = lax.axis_size("lon"), lax.axis_size("lat")
    return (
        passed(lon_strip, "lon", (n_lon,), (by,)),
        passed(lat_strip, "lat", (n_lat,), (by,)),
        passed(corner, ("lon", "lat"), (n_lon, n_lat), (by, by)),
    )


STRIPS = [((2, 2, 18, 8, C), BF16), ((2, 2, 3, 24, C), BF16), ((2, 2, 3, 8, C), BF16)]


def run_shadow(lat, bias_table, norm_gain, project_in, project_out, mask_ids):
    return call(
        shadow_kernel,
        [
            ((TAB * HEADS, POINTS, POINTS), F32),
            ((3 * C, C), BF16),
            ((C, C), BF16),
            ((C, POINTS), F32),
            ((TAB, 2, 1, POINTS), F32),
        ],
        (
            lat, bias_table.transpose(1, 0, 2), norm_gain.reshape(1, C), project_in, project_out,
            mask_ids.transpose(1, 0, 2),
        ),
        [((TAB, HEADS, ENTRIES), F32), ((TAB, 96, 384), F32), ((TAB, 16, 128), F32)],
        56,
    )


SUMS = [
    ((2, 2, 384, C), F32),
    ((C, 3 * C), F32),
    ((C, C), F32),
    ((C, POINTS), F32),
    ((2 * HEADS, POINTS, POINTS), F32),
]


def run_main(me, x, y, strips, regions, gain, project_in, win_t, project_out, wout_t, bias):
    weights = (
        near(regions), near(gain), project_in, near(win_t), project_out, near(wout_t), near(bias),
    )
    inner = call(inner_kernel, SUMS, (x, y, *weights), [((2, 2, 15, 32, C), F32)], 50)
    return call(
        main_kernel,
        [((2, 18, 24, C), BF16)] * 2 + STRIPS[:2] + [((16, CHUNK, 128), F32), ((16, CHUNK, 128), BF16)],
        (me, x, y, *map(near, strips), *weights, *map(near, inner)),
        [
            ((2, 2, 21, 32, C), F32),
            ((C, 4 * C), F32),
            ((C, C), F32),
            ((C, POINTS), F32),
            ((TAB * HEADS, POINTS, POINTS), F32),
            ((TAB * HEADS * 16, POINTS), F32),
            ((96, 384), F32),
            ((TAB * 8, LANE_BLOCKS * 128), F32),
            ((32 * T_ROWS, 128), F32),
            ((2, 16, CHUNK, 128), F32),
        ],
        46,
    )


def local(inputs, cotangent, mask_ids, norm_gain, project_in, project_out, bias_table):
    x, y = inputs[0], cotangent[0]
    lat = lax.axis_index("lat").astype(I32).reshape(1)
    me = lax.axis_index("ens").astype(I32).reshape(1)
    strips = halo(*call(strips_kernel, STRIPS, (x, y), (), 56), -1)
    bias, win_t, wout_t, gain, regions = run_shadow(lat, bias_table, norm_gain, project_in, project_out, mask_ids)
    out, in_grad, lon_s, lat_s, keep, send = run_main(
        me, x, y, strips, regions, gain, project_in, win_t, project_out, wout_t, bias
    )
    got = passed(send, "ens", (2,), (1,))
    (part,) = call(over_ens_kernel, [((16, CHUNK, 128), BF16)], (near(keep), near(got)))
    part = lax.all_to_all(part, "lon", 0, 0, tiled=True)
    (part,) = call(over_lon_kernel, [((8, CHUNK, 128), BF16)], (near(part),))
    lon_s = passed(lon_s, "lon", (lax.axis_size("lon"),), (1,))
    part = lax.all_to_all(part, "lat", 0, 0, tiled=True)
    part, lat_s = call(
        over_lat_kernel,
        [((16, SHARD, 128), BF16), STRIPS[1]],
        (near(part), near(lon_s), near(lat_s)),
    )
    lat_s = passed(lat_s, "lat", (lax.axis_size("lat"),), (1,))
    mine = lax.all_to_all(part, "lon", 0, 0, tiled=True)
    mine, lat_s = lax.optimization_barrier((mine, lat_s))
    other = passed(mine, "ens", (2,), (1,))
    in_total, out_total, gain_total, table_total = call(
        final_kernel,
        [
            ((C, 3 * C), F32, None),
            ((C, C), F32, None),
            ((1, C), F32, None),
            ((HEADS, 24, ENTRIES), F32, None),
        ],
        (me, near(mine), near(other)),
        [
            ((2, 16, SHARD, 128), F32),
            ((8, 32 * T_ROWS, 128), F32),
            ((C, 4 * C), F32),
            ((144, LANE_BLOCKS * 128), F32),
        ],
    )
    out, in_grad = call(
        place_kernel,
        [((2, 18, 24, C), BF16, None)] * 2,
        (near(out), near(in_grad), near(lon_s), near(lat_s)),
    )
    return (
        out[None],
        in_grad[None],
        in_total,
        out_total,
        gain_total.reshape(C),
        table_total.transpose(1, 0, 2),
    )


def solution(mesh):
    return jax.shard_map(
        local,
        mesh=mesh,
        in_specs=(
            P("ens", None, "lat", "lon", None),
            P("ens", None, "lat", "lon", None),
            P(None, "lat", "lon"),
            P(),
            P(),
            P(),
            P(),
        ),
        out_specs=(
            P("ens", None, "lat", "lon", None),
            P("ens", None, "lat", "lon", None),
            P(),
            P(),
            P(),
            P(),
        ),
        check_vma=False,
    )
```

```python
import jax
import jax.numpy as jnp
from jax import lax
from jax.experimental import pallas as pl
from jax.experimental.pallas import tpu as pltpu
from jax.sharding import PartitionSpec as P

WL, WLAT, WLON = 2, 6, 12
AB = WL * WLAT
POINTS = AB * WLON
SPAN = 2 * WLON - 1
EPS = 1e-05
F32, BF16, I32 = jnp.float32, jnp.bfloat16, jnp.int32
C, HEADS, HD = 192, 6, 32
FACTOR = HD ** (-0.5)
TAB = 3
ENTRIES = AB * AB * SPAN
LANE_BLOCKS = -(-ENTRIES // 128)
CHUNK = 64
G_ROWS = 40
T_ROWS = 16
SHARD = 168


def dot(a, b, ca, cb):
    return lax.dot_general(a, b, (((ca,), (cb,)), ((), ())), preferred_element_type=F32)


def iota(shape, dim):
    return lax.broadcasted_iota(I32, shape, dim)


def segments():
    for ab_p in range(AB):
        a_p, b_p = divmod(ab_p, WLAT)
        for ab_r in range(AB):
            a_r, b_r = divmod(ab_r, WLAT)
            yield ab_p, ab_r, (((a_p * WL + a_r) * WLAT + b_p) * WLAT + b_r) * SPAN


def tokens():
    p = iota((1, POINTS), 1)
    c_p = (p * 21846) >> 18
    return c_p, p - c_p * AB


def toeplitz(c):
    c_p, ab_p = tokens()
    return (iota((384, POINTS), 0) == ab_p * SPAN + c_p + (WLON - 1 - c)).astype(BF16)


def heads_first():
    n = iota((96, 96), 0)
    return ((iota((96, 96), 1) == (n & 15) * 8 + (n >> 4)) & ((n & 15) < AB)).astype(BF16)


def prepare_kernel(
    lat_ref, x_ref, y_ref, table_ref, gain_ref, win_ref, wout_ref, mask_ref,
    lon_out, lat_out, cor_out, x_out, y_out, bias_ref, win_out, win_t_ref, wout_out, wout_t_ref, gain_out, region_ref,
    own_ref, rows_ref, ids_ref,
):
    for k, (ref, copy) in enumerate(((x_ref, x_out), (y_ref, y_out))):
        lon_out[k] = ref[:, :, 0:8, :]
        lat_out[k] = ref[:, 0:3, :, :]
        cor_out[k] = ref[:, 0:3, 0:8, :]
        copy[...] = ref[...]
    win_out[...] = win_ref[...]
    wout_out[...] = wout_ref[...]
    first = lat_ref[0] * TAB
    for t in range(TAB):
        for h in range(HEADS):
            own_ref[t, h : h + 1, :] = table_ref[h, pl.ds(first + t, 1), :]
    rows_ref[...] = jnp.zeros_like(rows_ref)
    for t in range(TAB):
        for ab_p, ab_r, start in segments():
            rows_ref[t, ab_r * 8 : ab_r * 8 + HEADS, ab_p * SPAN : (ab_p + 1) * SPAN] = own_ref[
                t, :, start : start + SPAN
            ]
    order = heads_first()
    m = iota((1, 384), 1)
    x = (m * 21846) >> 18
    swap = (iota((384, 384), 0) == (m - x * AB) * SPAN + x).astype(BF16)
    full = 0.0
    rest = [rows_ref[t] for t in range(TAB)]
    for _ in range(3):
        low = [r.astype(BF16) for r in rest]
        rest = [r - p.astype(F32) for r, p in zip(rest, low)]
        full = full + dot(jnp.concatenate([dot(order, p, 1, 0).astype(BF16) for p in low], axis=0), swap, 1, 0)
    for c in range(WLON):
        start = (WLON - 1 - c) * AB
        part = full[:, start : start + POINTS]
        for th in range(TAB * HEADS):
            bias_ref[th, c * AB : (c + 1) * AB, :] = part[th * 16 : th * 16 + AB, :]
    win_t_ref[...] = win_ref[...].T
    wout_t_ref[...] = wout_ref[...].T
    column = jnp.broadcast_to(gain_ref[...], (8, C)).T
    gain_out[...] = jnp.broadcast_to(column[:, 0:1], (C, POINTS))
    ids_ref[...] = jnp.zeros_like(ids_ref)
    c_p, ab_p = tokens()
    for v in range(TAB):
        for b in range(WLAT):
            for a in range(WL):
                at = a * WLAT + b
                ids_ref[v, at : at + 1, 0:24] = mask_ref[v * WLAT + b, a : a + 1, :].astype(F32)
        for w in range(2):
            pick = (iota((128, POINTS), 0) == c_p + WLON * w).astype(BF16)
            spread = dot(ids_ref[v].astype(BF16), pick, 1, 0)
            own = jnp.where(iota((16, POINTS), 0) == ab_p, spread, 0.0)
            region_ref[v, w] = jnp.sum(own, axis=0, keepdims=True)


def windows(weights, sums, save):
    region_ref, gain_ref, win_ref, win_t_ref, wout_ref, wout_t_ref, bias_ref = weights
    grads, outer, gain_acc = sums
    gain = gain_ref[...]
    heads = [(iota((POINTS, C), 1) >> 5) == h for h in range(HEADS)]
    c_p, ab_p = tokens()
    level = jnp.where(ab_p >= WLAT, 1, 0)
    place = (1 - level) * (WLAT * 32) + (ab_p - level * WLAT) * 32 + WLON // 2 + c_p

    def window(v, w, x_rows, y_rows):
        pick = (iota((384, POINTS), 0) == place + WLON * w).astype(BF16)
        xt = dot(x_rows, pick, 1, 0)
        ct32 = dot(y_rows, pick, 1, 0)
        yield
        ct = ct32.astype(BF16)
        center = xt - jnp.mean(xt, axis=0, keepdims=True)
        inverse = lax.rsqrt(jnp.mean(center * center, axis=0, keepdims=True) + EPS)
        part = center * inverse
        normed = (part * gain).astype(BF16)
        yield
        triple = dot(win_t_ref[...], normed, 1, 0).astype(BF16)
        grad_mixed = dot(wout_ref[...], ct, 1, 0).astype(BF16)
        yield
        natural = dot(normed, win_ref[...], 0, 0).astype(BF16)
        gm_n = dot(ct, wout_t_ref[...], 0, 0).astype(BF16)
        ids = region_ref[v, w]
        member = (iota((8, POINTS), 0).astype(F32) == ids).astype(BF16)
        barred = (dot(member, member, 0, 0) - 1.0) * 1e30
        yield
        q_n, k_n, v_n = natural[:, :C], natural[:, C : 2 * C], natural[:, 2 * C :]
        zero = jnp.zeros_like(k_n)
        k_heads = jnp.concatenate([jnp.where(m, k_n, zero) for m in heads], axis=0)
        v_heads = jnp.concatenate([jnp.where(m, v_n, zero) for m in heads], axis=0)
        all_scores = dot(k_heads, triple[:C], 1, 0)
        all_g_prob = dot(v_heads, grad_mixed, 1, 0)
        yield
        mixed, g_q, lows, g_lows = [], [], [], []
        for h in range(HEADS):
            lo, hi = h * HD, (h + 1) * HD
            part_h = slice(h * POINTS, (h + 1) * POINTS)
            scores = all_scores[part_h] * FACTOR + (bias_ref[v * HEADS + h] + barred)
            raised = jnp.exp(scores - jnp.max(scores, axis=0, keepdims=True))
            prob = raised * (1.0 / jnp.sum(raised, axis=0, keepdims=True))
            low = prob.astype(BF16)
            mixed.append(dot(triple[2 * C + lo : 2 * C + hi], low, 1, 0))
            g_prob = all_g_prob[part_h]
            g_score = prob * (g_prob - jnp.sum(prob * g_prob, axis=0, keepdims=True))
            save(v, w, h, g_score)
            g_low = g_score.astype(BF16)
            g_q.append(dot(triple[C + lo : C + hi], g_low, 1, 0) * FACTOR)
            lows.append(low)
            g_lows.append(g_low)
            yield
        all_g_v = dot(jnp.concatenate(lows, axis=0), gm_n, 1, 0)
        all_g_k = dot(jnp.concatenate(g_lows, axis=0), q_n, 1, 0)
        mixed = jnp.concatenate(mixed, axis=0).astype(BF16)
        attended = dot(wout_t_ref[...], mixed, 1, 0).astype(BF16)
        outer[...] += dot(mixed, ct, 1, 1)
        yield
        g_v, g_k = all_g_v[:POINTS], all_g_k[:POINTS]
        for h in range(1, HEADS):
            part_h = slice(h * POINTS, (h + 1) * POINTS)
            g_v = jnp.where(heads[h], all_g_v[part_h], g_v)
            g_k = jnp.where(heads[h], all_g_k[part_h], g_k)
        g_q = jnp.concatenate(g_q, axis=0).astype(BF16)
        g_k = (g_k * FACTOR).astype(BF16)
        g_v = g_v.astype(BF16)
        wide = dot(win_ref[:, :C], g_q, 1, 0)
        wide = wide + dot(win_ref[:, C : 2 * C], g_k, 1, 1) + dot(win_ref[:, 2 * C :], g_v, 1, 1)
        wide = wide.astype(BF16).astype(F32)
        yield
        grads[:, :C] += dot(normed, g_q, 1, 1)
        grads[:, C : 2 * C] += dot(normed, g_k, 1, 0)
        grads[:, 2 * C : 3 * C] += dot(normed, g_v, 1, 0)
        block = (xt + attended.astype(F32)).astype(BF16)
        gain_acc[...] += wide * part
        scaled = wide * gain
        grad_part = inverse * (
            scaled
            - jnp.mean(scaled, axis=0, keepdims=True)
            - part * jnp.mean(scaled * part, axis=0, keepdims=True)
        )
        in_grad = (ct32 + grad_part).astype(BF16)
        yield
        yield dot(pick, block, 1, 1), dot(pick, in_grad, 1, 1)

    return window


def interleaved(window, ext, chosen):
    def rows_of(k, v):
        return ext[k, :, 6 * v + 3 : 6 * v + 9].reshape(384, C).astype(BF16).T

    results = [None]
    todo = [window(v, w, rows_of(0, v), rows_of(1, v)) for v, w in chosen]
    while results[0] is None:
        results = [next(g) for g in todo]
    return dict(zip(chosen, results))


def inner_kernel(
    x_ref, y_ref, region_ref, gain_ref, win_ref, win_t_ref, wout_ref, wout_t_ref, bias_ref,
    rows_ref, grads, outer, gain_acc, dbias, ext,
):
    for k, ref in enumerate((x_ref, y_ref)):
        ext[k, :, :, 0:24, :] = ref[:, 0:15].astype(F32)
        ext[k, :, :, 24:32, :] = jnp.zeros((2, 15, 8, C), F32)
    for ref in (grads, outer, gain_acc):
        ref[...] = jnp.zeros_like(ref)

    def save(v, w, h, g_score):
        dbias[v * HEADS + h] = g_score

    weights = (region_ref, gain_ref, win_ref, win_t_ref, wout_ref, wout_t_ref, bias_ref)
    got = interleaved(windows(weights, (grads, outer, gain_acc), save), ext, [(0, 0), (1, 0)])
    for v in range(2):
        for k in range(2):
            rows_ref[k, v] = got[v, 0][k]


def main_kernel(
    ens_ref, x_ref, y_ref, lon_ref, lat_ref, cor_ref, region_ref, gain_ref, win_ref, win_t_ref, wout_ref,
    wout_t_ref, bias_ref, rows_in, grads_in, outer_in, gain_in, dbias_in,
    out_ref, ig_ref, lon_out, lat_out, keep_ref, send_ref,
    ext, grads, outer, gain_acc, dbias, blocks, rows, flat_t, flat, chunks,
):
    for k, ref in enumerate((x_ref, y_ref)):
        ext[k, :, 0:18, 0:24, :] = ref[...].astype(F32)
        ext[k, :, 0:18, 24:32, :] = lon_ref[k].astype(F32)
        ext[k, :, 18:21, 0:24, :] = lat_ref[k].astype(F32)
        ext[k, :, 18:21, 24:32, :] = cor_ref[k].astype(F32)
    grads[:, : 3 * C] = grads_in[...]
    outer[...] = outer_in[...]
    gain_acc[...] = gain_in[...]

    def save(v, w, h, g_score):
        at = v * HEADS + h
        if v < 2:
            dbias[at] = dbias_in[at] + g_score
        elif w == 0:
            dbias[at] = g_score
        else:
            dbias[at] += g_score

    weights = (region_ref, gain_ref, win_ref, win_t_ref, wout_ref, wout_t_ref, bias_ref)
    got = interleaved(
        windows(weights, (grads, outer, gain_acc), save), ext, [(0, 1), (1, 1), (2, 0), (2, 1)]
    )
    for v in range(TAB):
        for k in range(2):
            first = rows_in[k, v] if v < 2 else got[v, 0][k]
            ext[k, :, 6 * v + 3 : 6 * v + 9] = (first + got[v, 1][k]).reshape(2, 6, 32, C)
    for k, ref in enumerate((out_ref, ig_ref)):
        ext[k, :, 0:3] = jnp.zeros((2, 3, 32, C), F32)
        ref[...] = ext[k, :, 0:18, 0:24, :].astype(BF16)
        lon_out[k] = ext[k, :, 3:21, 24:32, :].astype(BF16)
        lat_out[k] = ext[k, :, 18:21, 0:24, :].astype(BF16)

    blocks[...] = jnp.zeros_like(blocks)
    total = jnp.zeros((TAB * HEADS * 16, 384), F32)
    for c in range(WLON):
        for th in range(TAB * HEADS):
            blocks[th * 16 : th * 16 + AB, :] = dbias[th, c * AB : (c + 1) * AB, :]
        total = total + dot(blocks[...].astype(BF16), toeplitz(c), 1, 1)
    flat_t[...] = jnp.zeros_like(flat_t)
    for t in range(TAB):
        rows[...] = dot(heads_first(), total[t * 96 : (t + 1) * 96].astype(BF16), 0, 0)
        for ab_p, ab_r, start in segments():
            flat_t[t * 8 : t * 8 + 8, start : start + SPAN] = rows[
                ab_r * 8 : ab_r * 8 + 8, ab_p * SPAN : (ab_p + 1) * SPAN
            ]
    flat[...] = jnp.zeros_like(flat)
    for block in range(LANE_BLOCKS):
        for t in range(TAB):
            at = (block * TAB + t) * HEADS
            flat[at : at + HEADS, :] = flat_t[t * 8 : t * 8 + HEADS, block * 128 : (block + 1) * 128]

    chunks[...] = jnp.zeros_like(chunks)
    grads[:, 3 * C :] = outer[...]
    tile = 0
    for group in range(C // 8):
        for block in range(C * 4 // 128):
            chunk, slot = divmod(tile, G_ROWS // 8)
            chunks[chunk // 16, chunk % 16, slot * 8 : slot * 8 + 8, :] = grads[
                group * 8 : group * 8 + 8, block * 128 : (block + 1) * 128
            ]
            tile += 1
    for chunk in range(32):
        chunks[chunk // 16, chunk % 16, G_ROWS : G_ROWS + T_ROWS, :] = flat[chunk * T_ROWS : (chunk + 1) * T_ROWS]
    rest = gain_acc[...]
    gain_row = jnp.zeros((8, C), F32)
    for _ in range(3):
        low = rest.astype(BF16)
        rest = rest - low.astype(F32)
        gain_row = gain_row + dot(jnp.ones((8, POINTS), BF16), low, 1, 1)
    chunks[1, 13, 0:1, :] = gain_row[0:1, 0:128]
    chunks[1, 13, 1:2, 0:64] = gain_row[0:1, 128:192]
    me = ens_ref[0]
    keep_ref[...] = chunks[me]
    send_ref[...] = chunks[1 - me].astype(BF16)


def over_ens_kernel(keep_ref, got_ref, out_ref):
    out_ref[...] = (keep_ref[...] + got_ref[...].astype(F32)).astype(BF16)


def over_lon_kernel(got_ref, out_ref):
    total = jnp.sum(got_ref[...].astype(F32), axis=0).astype(BF16)
    for k in range(out_ref.shape[0]):
        out_ref[k] = total


def over_lat_kernel(got_ref, lon_ref, lat_ref, out_ref, lat_out):
    lat_out[:, :, :, 8:24, :] = lat_ref[:, :, :, 8:24, :]
    corner = lat_ref[:, :, :, 0:8, :].astype(F32) + lon_ref[:, :, 15:18].astype(F32)
    lat_out[:, :, :, 0:8, :] = corner.astype(BF16)
    got = got_ref[...].astype(F32)
    total = jnp.sum(got[:, :G_ROWS], axis=0)
    shard = jnp.concatenate([total] + [got[k, G_ROWS : G_ROWS + T_ROWS] for k in range(8)], axis=0).astype(BF16)
    for k in range(out_ref.shape[0]):
        out_ref[k] = shard


def place_kernel(out_ref, grad_ref, lon_ref, lat_ref, out_whole, grad_whole):
    for k, (ref, whole) in enumerate(((out_ref, out_whole), (grad_ref, grad_whole))):
        left = ref[:, 3:, 0:8, :].astype(F32) + lon_ref[k, :, 0:15].astype(F32)
        whole[:, 3:, 0:8, :] = left.astype(BF16)
        whole[:, 3:, 8:24, :] = ref[:, 3:, 8:24, :]
        whole[:, 0:3] = lat_ref[k]


def final_kernel(ens_ref, mine_ref, other_ref, in_ref, outer_ref, gain_ref, table_ref, both, tables, grads, full):
    me = ens_ref[0]
    both[me] = mine_ref[...].astype(F32)
    both[1 - me] = other_ref[...].astype(F32)
    tile = 0
    for group in range(C // 8):
        for block in range(C * 4 // 128):
            chunk, slot = divmod(tile, G_ROWS // 8)
            grads[group * 8 : group * 8 + 8, block * 128 : (block + 1) * 128] = both[
                chunk // 16, chunk % 16, slot * 8 : slot * 8 + 8, :
            ]
            tile += 1
    in_ref[...] = grads[:, 0 : 3 * C]
    outer_ref[...] = grads[:, 3 * C :]
    gain_ref[0:1, 0:128] = both[1, 13, 0:1, :]
    gain_ref[0:1, 128:192] = both[1, 13, 1:2, 0:64]
    for lat in range(8):
        for chunk in range(32):
            tables[lat, chunk * T_ROWS : (chunk + 1) * T_ROWS, :] = both[
                chunk // 16, chunk % 16, G_ROWS + lat * T_ROWS : G_ROWS + (lat + 1) * T_ROWS, :
            ]
    count = TAB * HEADS
    for lat in range(8):
        for block in range(LANE_BLOCKS):
            full[lat * count : (lat + 1) * count, block * 128 : (block + 1) * 128] = tables[
                lat, block * count : (block + 1) * count, :
            ]
    m = iota((144, 144), 0)
    h24 = (m * 43691) >> 20
    order = (iota((144, 144), 1) == (m - h24 * 24) * HEADS + h24).astype(BF16)
    ordered = dot(order, full[...].astype(BF16), 1, 0)
    for h in range(HEADS):
        table_ref[h] = ordered[h * 24 : (h + 1) * 24, :ENTRIES]


SMEM = pl.BlockSpec(memory_space=pltpu.SMEM)
WHOLE = pl.BlockSpec(memory_space=pltpu.VMEM)


def call(kernel, outs, args, scratch=(), room=24):
    specs = [SMEM if a.dtype == I32 and a.ndim == 1 else WHOLE for a in args]
    shapes = tuple(pltpu.VMEM(*o) if len(o) == 2 else jax.ShapeDtypeStruct(*o[:2]) for o in outs)
    return pl.pallas_call(
        kernel,
        out_shape=shapes,
        in_specs=specs,
        out_specs=tuple(WHOLE for _ in outs),
        scratch_shapes=[pltpu.VMEM(*x) for x in scratch],
        compiler_params=pltpu.CompilerParams(vmem_limit_bytes=room * 2**20),
    )(*args)


def near(x):
    return pltpu.with_memory_space_constraint(x, pltpu.VMEM)


def passed(x, axes, sizes, moves):
    total = [()]
    for size in sizes:
        total = [t + (i,) for t in total for i in range(size)]

    def number(index):
        n = 0
        for i, size in zip(index, sizes):
            n = n * size + i % size
        return n

    pairs = [(number(t), number(tuple(i + m for i, m in zip(t, moves)))) for t in total]
    return lax.ppermute(x, axes, pairs)


def halo(lon_strip, lat_strip, corner, by):
    n_lon, n_lat = lax.axis_size("lon"), lax.axis_size("lat")
    return (
        passed(lon_strip, "lon", (n_lon,), (by,)),
        passed(lat_strip, "lat", (n_lat,), (by,)),
        passed(corner, ("lon", "lat"), (n_lon, n_lat), (by, by)),
    )


STRIPS = [((2, 2, 18, 8, C), BF16), ((2, 2, 3, 24, C), BF16), ((2, 2, 3, 8, C), BF16)]


def run_prepare(lat, x, y, bias_table, norm_gain, project_in, project_out, mask_ids):
    return call(
        prepare_kernel,
        [
            *STRIPS,
            ((2, 18, 24, C), BF16),
            ((2, 18, 24, C), BF16),
            ((TAB * HEADS, POINTS, POINTS), F32),
            ((C, 3 * C), BF16),
            ((3 * C, C), BF16),
            ((C, C), BF16),
            ((C, C), BF16),
            ((C, POINTS), F32),
            ((TAB, 2, 1, POINTS), F32),
        ],
        (
            lat, x, y, bias_table.transpose(1, 0, 2), norm_gain.reshape(1, C), project_in, project_out,
            mask_ids.transpose(1, 0, 2),
        ),
        [((TAB, HEADS, ENTRIES), F32), ((TAB, 96, 384), F32), ((TAB, 16, 128), F32)],
        50,
    )


SUMS = [
    ((2, 2, 384, C), F32),
    ((C, 3 * C), F32),
    ((C, C), F32),
    ((C, POINTS), F32),
    ((2 * HEADS, POINTS, POINTS), F32),
]


def run_main(me, x, y, strips, weights):
    x, y, *weights = map(near, (x, y, *weights))
    inner = call(inner_kernel, SUMS, (x, y, *weights), [((2, 2, 15, 32, C), F32)], 50)
    return call(
        main_kernel,
        [((2, 18, 24, C), BF16)] * 2 + STRIPS[:2] + [((16, CHUNK, 128), F32), ((16, CHUNK, 128), BF16)],
        (me, x, y, *map(near, strips), *weights, *map(near, inner)),
        [
            ((2, 2, 21, 32, C), F32),
            ((C, 4 * C), F32),
            ((C, C), F32),
            ((C, POINTS), F32),
            ((TAB * HEADS, POINTS, POINTS), F32),
            ((TAB * HEADS * 16, POINTS), F32),
            ((96, 384), F32),
            ((TAB * 8, LANE_BLOCKS * 128), F32),
            ((32 * T_ROWS, 128), F32),
            ((2, 16, CHUNK, 128), F32),
        ],
        46,
    )


def local(inputs, cotangent, mask_ids, norm_gain, project_in, project_out, bias_table):
    x, y = inputs[0], cotangent[0]
    lat = lax.axis_index("lat").astype(I32).reshape(1)
    me = lax.axis_index("ens").astype(I32).reshape(1)
    lon_s, lat_s, cor_s, x, y, bias, win, win_t, wout, wout_t, gain, regions = run_prepare(
        lat, x, y, bias_table, norm_gain, project_in, project_out, mask_ids
    )
    strips = halo(lon_s, lat_s, cor_s, -1)
    out, in_grad, lon_s, lat_s, keep, send = run_main(
        me, x, y, strips, (regions, gain, win, win_t, wout, wout_t, bias)
    )
    got = passed(send, "ens", (2,), (1,))
    (part,) = call(over_ens_kernel, [((16, CHUNK, 128), BF16)], (near(keep), near(got)))
    part = lax.all_to_all(part, "lon", 0, 0, tiled=True)
    (part,) = call(over_lon_kernel, [((8, CHUNK, 128), BF16)], (near(part),))
    lon_s = passed(lon_s, "lon", (lax.axis_size("lon"),), (1,))
    part = lax.all_to_all(part, "lat", 0, 0, tiled=True)
    part, lat_s = call(
        over_lat_kernel,
        [((16, SHARD, 128), BF16), STRIPS[1]],
        (near(part), near(lon_s), near(lat_s)),
    )
    lat_s = passed(lat_s, "lat", (lax.axis_size("lat"),), (1,))
    mine = lax.all_to_all(part, "lon", 0, 0, tiled=True)
    mine, lat_s = lax.optimization_barrier((mine, lat_s))
    other = passed(mine, "ens", (2,), (1,))
    in_total, out_total, gain_total, table_total = call(
        final_kernel,
        [
            ((C, 3 * C), F32, None),
            ((C, C), F32, None),
            ((1, C), F32, None),
            ((HEADS, 24, ENTRIES), F32, None),
        ],
        (me, near(mine), near(other)),
        [
            ((2, 16, SHARD, 128), F32),
            ((8, 32 * T_ROWS, 128), F32),
            ((C, 4 * C), F32),
            ((144, LANE_BLOCKS * 128), F32),
        ],
    )
    out, in_grad = call(
        place_kernel,
        [((2, 18, 24, C), BF16, None)] * 2,
        (near(out), near(in_grad), near(lon_s), near(lat_s)),
    )
    return (
        out[None],
        in_grad[None],
        in_total,
        out_total,
        gain_total.reshape(C),
        table_total.transpose(1, 0, 2),
    )


def solution(mesh):
    return jax.shard_map(
        local,
        mesh=mesh,
        in_specs=(
            P("ens", None, "lat", "lon", None),
            P("ens", None, "lat", "lon", None),
            P(None, "lat", "lon"),
            P(),
            P(),
            P(),
            P(),
        ),
        out_specs=(
            P("ens", None, "lat", "lon", None),
            P("ens", None, "lat", "lon", None),
            P(),
            P(),
            P(),
            P(),
        ),
        check_vma=False,
    )
```

```python
import jax
import jax.numpy as jnp
from jax import lax
from jax.experimental import pallas as pl
from jax.experimental.pallas import tpu as pltpu
from jax.sharding import PartitionSpec as P

WL, WLAT, WLON = 2, 6, 12
AB = WL * WLAT
POINTS = AB * WLON
SPAN = 2 * WLON - 1
EPS = 1e-05
F32, BF16, I32 = jnp.float32, jnp.bfloat16, jnp.int32
C, HEADS, HD = 192, 6, 32
FACTOR = HD ** (-0.5)
TAB = 3
ENTRIES = AB * AB * SPAN
LANE_BLOCKS = -(-ENTRIES // 128)
CHUNK = 64
G_ROWS = 40
T_ROWS = 16
SHARD = 168


def dot(a, b, ca, cb):
    return lax.dot_general(a, b, (((ca,), (cb,)), ((), ())), preferred_element_type=F32)


def iota(shape, dim):
    return lax.broadcasted_iota(I32, shape, dim)


def segments():
    for ab_p in range(AB):
        a_p, b_p = divmod(ab_p, WLAT)
        for ab_r in range(AB):
            a_r, b_r = divmod(ab_r, WLAT)
            yield ab_p, ab_r, (((a_p * WL + a_r) * WLAT + b_p) * WLAT + b_r) * SPAN


def tokens():
    p = iota((1, POINTS), 1)
    c_p = (p * 21846) >> 18
    return c_p, p - c_p * AB


def toeplitz(c):
    c_p, ab_p = tokens()
    return (iota((384, POINTS), 0) == ab_p * SPAN + c_p + (WLON - 1 - c)).astype(BF16)


def heads_first():
    n = iota((96, 96), 0)
    return ((iota((96, 96), 1) == (n & 15) * 8 + (n >> 4)) & ((n & 15) < AB)).astype(BF16)


def strips_kernel(x_ref, y_ref, lon_ref, lat_ref, cor_ref, x_out, y_out):
    for k, (ref, copy) in enumerate(((x_ref, x_out), (y_ref, y_out))):
        copy[...] = ref[...]
        lon_ref[k] = ref[:, :, 0:8, :]
        lat_ref[k] = ref[:, 0:3, :, :]
        cor_ref[k] = ref[:, 0:3, 0:8, :]


def shadow_kernel(
    lat_ref, table_ref, gain_ref, win_ref, wout_ref, mask_ref,
    bias_ref, win_t_ref, wout_t_ref, gain_out, region_ref, own_ref, rows_ref, ids_ref,
):
    first = lat_ref[0] * TAB
    for t in range(TAB):
        for h in range(HEADS):
            own_ref[t, h : h + 1, :] = table_ref[h, pl.ds(first + t, 1), :]
    rows_ref[...] = jnp.zeros_like(rows_ref)
    for t in range(TAB):
        for ab_p, ab_r, start in segments():
            rows_ref[t, ab_r * 8 : ab_r * 8 + HEADS, ab_p * SPAN : (ab_p + 1) * SPAN] = own_ref[
                t, :, start : start + SPAN
            ]
    order = heads_first()
    m = iota((1, 384), 1)
    x = (m * 21846) >> 18
    swap = (iota((384, 384), 0) == (m - x * AB) * SPAN + x).astype(BF16)
    full = 0.0
    rest = [rows_ref[t] for t in range(TAB)]
    for _ in range(3):
        low = [r.astype(BF16) for r in rest]
        rest = [r - p.astype(F32) for r, p in zip(rest, low)]
        full = full + dot(jnp.concatenate([dot(order, p, 1, 0).astype(BF16) for p in low], axis=0), swap, 1, 0)
    for c in range(WLON):
        start = (WLON - 1 - c) * AB
        part = full[:, start : start + POINTS]
        for th in range(TAB * HEADS):
            bias_ref[th, c * AB : (c + 1) * AB, :] = part[th * 16 : th * 16 + AB, :]
    win_t_ref[...] = win_ref[...].T
    wout_t_ref[...] = wout_ref[...].T
    column = jnp.broadcast_to(gain_ref[...], (8, C)).T
    gain_out[...] = jnp.broadcast_to(column[:, 0:1], (C, POINTS))
    ids_ref[...] = jnp.zeros_like(ids_ref)
    c_p, ab_p = tokens()
    for v in range(TAB):
        for b in range(WLAT):
            for a in range(WL):
                at = a * WLAT + b
                ids_ref[v, at : at + 1, 0:24] = mask_ref[v * WLAT + b, a : a + 1, :].astype(F32)
        for w in range(2):
            pick = (iota((128, POINTS), 0) == c_p + WLON * w).astype(BF16)
            spread = dot(ids_ref[v].astype(BF16), pick, 1, 0)
            own = jnp.where(iota((16, POINTS), 0) == ab_p, spread, 0.0)
            region_ref[v, w] = jnp.sum(own, axis=0, keepdims=True)


def windows(weights, sums, save):
    region_ref, gain_ref, win_ref, win_t_ref, wout_ref, wout_t_ref, bias_ref = weights
    grads, outer, gain_acc = sums
    gain = gain_ref[...]
    heads = [(iota((POINTS, C), 1) >> 5) == h for h in range(HEADS)]
    c_p, ab_p = tokens()
    level = jnp.where(ab_p >= WLAT, 1, 0)
    place = (1 - level) * (WLAT * 32) + (ab_p - level * WLAT) * 32 + WLON // 2 + c_p

    def window(v, w, x_rows, y_rows):
        pick = (iota((384, POINTS), 0) == place + WLON * w).astype(BF16)
        xt = dot(x_rows, pick, 1, 0)
        ct32 = dot(y_rows, pick, 1, 0)
        yield
        ct = ct32.astype(BF16)
        center = xt - jnp.mean(xt, axis=0, keepdims=True)
        inverse = lax.rsqrt(jnp.mean(center * center, axis=0, keepdims=True) + EPS)
        part = center * inverse
        normed = (part * gain).astype(BF16)
        yield
        triple = dot(win_t_ref[...], normed, 1, 0).astype(BF16)
        grad_mixed = dot(wout_ref[...], ct, 1, 0).astype(BF16)
        yield
        natural = dot(normed, win_ref[...], 0, 0).astype(BF16)
        gm_n = dot(ct, wout_t_ref[...], 0, 0).astype(BF16)
        ids = region_ref[v, w]
        member = (iota((8, POINTS), 0).astype(F32) == ids).astype(BF16)
        barred = (dot(member, member, 0, 0) - 1.0) * 1e30
        yield
        q_n, k_n, v_n = natural[:, :C], natural[:, C : 2 * C], natural[:, 2 * C :]
        zero = jnp.zeros_like(k_n)
        k_heads = jnp.concatenate([jnp.where(m, k_n, zero) for m in heads], axis=0)
        v_heads = jnp.concatenate([jnp.where(m, v_n, zero) for m in heads], axis=0)
        all_scores = dot(k_heads, triple[:C], 1, 0)
        all_g_prob = dot(v_heads, grad_mixed, 1, 0)
        yield
        mixed, g_q, lows, g_lows = [], [], [], []
        for h in range(HEADS):
            lo, hi = h * HD, (h + 1) * HD
            part_h = slice(h * POINTS, (h + 1) * POINTS)
            scores = all_scores[part_h] * FACTOR + (bias_ref[v * HEADS + h] + barred)
            raised = jnp.exp(scores - jnp.max(scores, axis=0, keepdims=True))
            prob = raised * (1.0 / jnp.sum(raised, axis=0, keepdims=True))
            low = prob.astype(BF16)
            mixed.append(dot(triple[2 * C + lo : 2 * C + hi], low, 1, 0))
            g_prob = all_g_prob[part_h]
            g_score = prob * (g_prob - jnp.sum(prob * g_prob, axis=0, keepdims=True))
            save(v, w, h, g_score)
            g_low = g_score.astype(BF16)
            g_q.append(dot(triple[C + lo : C + hi], g_low, 1, 0) * FACTOR)
            lows.append(low)
            g_lows.append(g_low)
            yield
        all_g_v = dot(jnp.concatenate(lows, axis=0), gm_n, 1, 0)
        all_g_k = dot(jnp.concatenate(g_lows, axis=0), q_n, 1, 0)
        mixed = jnp.concatenate(mixed, axis=0).astype(BF16)
        attended = dot(wout_t_ref[...], mixed, 1, 0).astype(BF16)
        outer[...] += dot(mixed, ct, 1, 1)
        yield
        g_v, g_k = all_g_v[:POINTS], all_g_k[:POINTS]
        for h in range(1, HEADS):
            part_h = slice(h * POINTS, (h + 1) * POINTS)
            g_v = jnp.where(heads[h], all_g_v[part_h], g_v)
            g_k = jnp.where(heads[h], all_g_k[part_h], g_k)
        g_q = jnp.concatenate(g_q, axis=0).astype(BF16)
        g_k = (g_k * FACTOR).astype(BF16)
        g_v = g_v.astype(BF16)
        wide = dot(win_ref[:, :C], g_q, 1, 0)
        wide = wide + dot(win_ref[:, C : 2 * C], g_k, 1, 1) + dot(win_ref[:, 2 * C :], g_v, 1, 1)
        wide = wide.astype(BF16).astype(F32)
        yield
        grads[:, :C] += dot(normed, g_q, 1, 1)
        grads[:, C : 2 * C] += dot(normed, g_k, 1, 0)
        grads[:, 2 * C : 3 * C] += dot(normed, g_v, 1, 0)
        block = (xt + attended.astype(F32)).astype(BF16)
        gain_acc[...] += wide * part
        scaled = wide * gain
        grad_part = inverse * (
            scaled
            - jnp.mean(scaled, axis=0, keepdims=True)
            - part * jnp.mean(scaled * part, axis=0, keepdims=True)
        )
        in_grad = (ct32 + grad_part).astype(BF16)
        yield
        yield dot(pick, block, 1, 1), dot(pick, in_grad, 1, 1)

    return window


def interleaved(window, ext, chosen):
    def rows_of(k, v):
        return ext[k, :, 6 * v + 3 : 6 * v + 9].reshape(384, C).astype(BF16).T

    results = [None]
    todo = [window(v, w, rows_of(0, v), rows_of(1, v)) for v, w in chosen]
    while results[0] is None:
        results = [next(g) for g in todo]
    return dict(zip(chosen, results))


def inner_kernel(
    x_ref, y_ref, region_ref, gain_ref, win_ref, win_t_ref, wout_ref, wout_t_ref, bias_ref,
    rows_ref, grads, outer, gain_acc, dbias, ext,
):
    for k, ref in enumerate((x_ref, y_ref)):
        ext[k, :, :, 0:24, :] = ref[:, 0:15].astype(F32)
        ext[k, :, :, 24:32, :] = jnp.zeros((2, 15, 8, C), F32)
    for ref in (grads, outer, gain_acc):
        ref[...] = jnp.zeros_like(ref)

    def save(v, w, h, g_score):
        dbias[v * HEADS + h] = g_score

    weights = (region_ref, gain_ref, win_ref, win_t_ref, wout_ref, wout_t_ref, bias_ref)
    got = interleaved(windows(weights, (grads, outer, gain_acc), save), ext, [(0, 0), (1, 0)])
    for v in range(2):
        for k in range(2):
            rows_ref[k, v] = got[v, 0][k].astype(BF16)


def main_kernel(
    ens_ref, x_ref, y_ref, lon_ref, lat_ref, cor_ref, region_ref, gain_ref, win_ref, win_t_ref, wout_ref,
    wout_t_ref, bias_ref, rows_in, grads_in, outer_in, gain_in, dbias_in,
    out_ref, ig_ref, lon_out, lat_out, keep_ref, send_ref,
    ext, grads, outer, gain_acc, dbias, blocks, rows, flat_t, flat, chunks,
):
    for k, ref in enumerate((x_ref, y_ref)):
        ext[k, :, 0:18, 0:24, :] = ref[...].astype(F32)
        ext[k, :, 0:18, 24:32, :] = lon_ref[k].astype(F32)
        ext[k, :, 18:21, 0:24, :] = lat_ref[k].astype(F32)
        ext[k, :, 18:21, 24:32, :] = cor_ref[k].astype(F32)
    grads[:, : 3 * C] = grads_in[...]
    outer[...] = outer_in[...]
    gain_acc[...] = gain_in[...]

    def save(v, w, h, g_score):
        at = v * HEADS + h
        if v < 2:
            dbias[at] = dbias_in[at] + g_score
        elif w == 0:
            dbias[at] = g_score
        else:
            dbias[at] += g_score

    weights = (region_ref, gain_ref, win_ref, win_t_ref, wout_ref, wout_t_ref, bias_ref)
    got = interleaved(
        windows(weights, (grads, outer, gain_acc), save), ext, [(0, 1), (1, 1), (2, 0), (2, 1)]
    )
    for v in range(TAB):
        for k in range(2):
            first = rows_in[k, v].astype(F32) if v < 2 else got[v, 0][k]
            ext[k, :, 6 * v + 3 : 6 * v + 9] = (first + got[v, 1][k]).reshape(2, 6, 32, C)
    for k, ref in enumerate((out_ref, ig_ref)):
        ext[k, :, 0:3] = jnp.zeros((2, 3, 32, C), F32)
        ref[...] = ext[k, :, 0:18, 0:24, :].astype(BF16)
        lon_out[k] = ext[k, :, 3:21, 24:32, :].astype(BF16)
        lat_out[k] = ext[k, :, 18:21, 0:24, :].astype(BF16)

    blocks[...] = jnp.zeros_like(blocks)
    total = jnp.zeros((TAB * HEADS * 16, 384), F32)
    for c in range(WLON):
        for th in range(TAB * HEADS):
            blocks[th * 16 : th * 16 + AB, :] = dbias[th, c * AB : (c + 1) * AB, :]
        total = total + dot(blocks[...].astype(BF16), toeplitz(c), 1, 1)
    flat_t[...] = jnp.zeros_like(flat_t)
    for t in range(TAB):
        rows[...] = dot(heads_first(), total[t * 96 : (t + 1) * 96].astype(BF16), 0, 0)
        for ab_p, ab_r, start in segments():
            flat_t[t * 8 : t * 8 + 8, start : start + SPAN] = rows[
                ab_r * 8 : ab_r * 8 + 8, ab_p * SPAN : (ab_p + 1) * SPAN
            ]
    flat[...] = jnp.zeros_like(flat)
    for block in range(LANE_BLOCKS):
        for t in range(TAB):
            at = (block * TAB + t) * HEADS
            flat[at : at + HEADS, :] = flat_t[t * 8 : t * 8 + HEADS, block * 128 : (block + 1) * 128]

    chunks[...] = jnp.zeros_like(chunks)
    grads[:, 3 * C :] = outer[...]
    tile = 0
    for group in range(C // 8):
        for block in range(C * 4 // 128):
            chunk, slot = divmod(tile, G_ROWS // 8)
            chunks[chunk // 16, chunk % 16, slot * 8 : slot * 8 + 8, :] = grads[
                group * 8 : group * 8 + 8, block * 128 : (block + 1) * 128
            ]
            tile += 1
    for chunk in range(32):
        chunks[chunk // 16, chunk % 16, G_ROWS : G_ROWS + T_ROWS, :] = flat[chunk * T_ROWS : (chunk + 1) * T_ROWS]
    rest = gain_acc[...]
    gain_row = jnp.zeros((8, C), F32)
    for _ in range(3):
        low = rest.astype(BF16)
        rest = rest - low.astype(F32)
        gain_row = gain_row + dot(jnp.ones((8, POINTS), BF16), low, 1, 1)
    chunks[1, 13, 0:1, :] = gain_row[0:1, 0:128]
    chunks[1, 13, 1:2, 0:64] = gain_row[0:1, 128:192]
    me = ens_ref[0]
    keep_ref[...] = chunks[me]
    send_ref[...] = chunks[1 - me].astype(BF16)


def over_ens_kernel(keep_ref, got_ref, out_ref):
    out_ref[...] = (keep_ref[...] + got_ref[...].astype(F32)).astype(BF16)


def over_lon_kernel(got_ref, out_ref):
    total = jnp.sum(got_ref[...].astype(F32), axis=0).astype(BF16)
    for k in range(out_ref.shape[0]):
        out_ref[k] = total


def over_lat_kernel(got_ref, lon_ref, lat_ref, out_ref, lat_out):
    lat_out[:, :, :, 8:24, :] = lat_ref[:, :, :, 8:24, :]
    corner = lat_ref[:, :, :, 0:8, :].astype(F32) + lon_ref[:, :, 15:18].astype(F32)
    lat_out[:, :, :, 0:8, :] = corner.astype(BF16)
    got = got_ref[...].astype(F32)
    total = jnp.sum(got[:, :G_ROWS], axis=0)
    shard = jnp.concatenate([total] + [got[k, G_ROWS : G_ROWS + T_ROWS] for k in range(8)], axis=0).astype(BF16)
    for k in range(out_ref.shape[0]):
        out_ref[k] = shard


def place_kernel(out_ref, grad_ref, lon_ref, lat_ref, out_whole, grad_whole):
    for k, (ref, whole) in enumerate(((out_ref, out_whole), (grad_ref, grad_whole))):
        left = ref[:, 3:, 0:8, :].astype(F32) + lon_ref[k, :, 0:15].astype(F32)
        whole[:, 3:, 0:8, :] = left.astype(BF16)
        whole[:, 3:, 8:24, :] = ref[:, 3:, 8:24, :]
        whole[:, 0:3] = lat_ref[k]


def final_kernel(ens_ref, mine_ref, other_ref, in_ref, outer_ref, gain_ref, table_ref, both, tables, grads, full):
    me = ens_ref[0]
    both[me] = mine_ref[...].astype(F32)
    both[1 - me] = other_ref[...].astype(F32)
    tile = 0
    for group in range(C // 8):
        for block in range(C * 4 // 128):
            chunk, slot = divmod(tile, G_ROWS // 8)
            grads[group * 8 : group * 8 + 8, block * 128 : (block + 1) * 128] = both[
                chunk // 16, chunk % 16, slot * 8 : slot * 8 + 8, :
            ]
            tile += 1
    in_ref[...] = grads[:, 0 : 3 * C]
    outer_ref[...] = grads[:, 3 * C :]
    gain_ref[0:1, 0:128] = both[1, 13, 0:1, :]
    gain_ref[0:1, 128:192] = both[1, 13, 1:2, 0:64]
    for lat in range(8):
        for chunk in range(32):
            tables[lat, chunk * T_ROWS : (chunk + 1) * T_ROWS, :] = both[
                chunk // 16, chunk % 16, G_ROWS + lat * T_ROWS : G_ROWS + (lat + 1) * T_ROWS, :
            ]
    count = TAB * HEADS
    for lat in range(8):
        for block in range(LANE_BLOCKS):
            full[lat * count : (lat + 1) * count, block * 128 : (block + 1) * 128] = tables[
                lat, block * count : (block + 1) * count, :
            ]
    m = iota((144, 144), 0)
    h24 = (m * 43691) >> 20
    order = (iota((144, 144), 1) == (m - h24 * 24) * HEADS + h24).astype(BF16)
    ordered = dot(order, full[...].astype(BF16), 1, 0)
    for h in range(HEADS):
        table_ref[h] = ordered[h * 24 : (h + 1) * 24, :ENTRIES]


SMEM = pl.BlockSpec(memory_space=pltpu.SMEM)
WHOLE = pl.BlockSpec(memory_space=pltpu.VMEM)


def call(kernel, outs, args, scratch=(), room=24):
    specs = [SMEM if a.dtype == I32 and a.ndim == 1 else WHOLE for a in args]
    shapes = tuple(pltpu.VMEM(*o) if len(o) == 2 else jax.ShapeDtypeStruct(*o[:2]) for o in outs)
    return pl.pallas_call(
        kernel,
        out_shape=shapes,
        in_specs=specs,
        out_specs=tuple(WHOLE for _ in outs),
        scratch_shapes=[pltpu.VMEM(*x) for x in scratch],
        compiler_params=pltpu.CompilerParams(vmem_limit_bytes=room * 2**20),
    )(*args)


def near(x):
    return pltpu.with_memory_space_constraint(x, pltpu.VMEM)


def passed(x, axes, sizes, moves):
    total = [()]
    for size in sizes:
        total = [t + (i,) for t in total for i in range(size)]

    def number(index):
        n = 0
        for i, size in zip(index, sizes):
            n = n * size + i % size
        return n

    pairs = [(number(t), number(tuple(i + m for i, m in zip(t, moves)))) for t in total]
    return lax.ppermute(x, axes, pairs)


def halo(lon_strip, lat_strip, corner, by):
    n_lon, n_lat = lax.axis_size("lon"), lax.axis_size("lat")
    return (
        passed(lon_strip, "lon", (n_lon,), (by,)),
        passed(lat_strip, "lat", (n_lat,), (by,)),
        passed(corner, ("lon", "lat"), (n_lon, n_lat), (by, by)),
    )


STRIPS = [((2, 2, 18, 8, C), BF16), ((2, 2, 3, 24, C), BF16), ((2, 2, 3, 8, C), BF16)]


def run_shadow(lat, bias_table, norm_gain, project_in, project_out, mask_ids):
    return call(
        shadow_kernel,
        [
            ((TAB * HEADS, POINTS, POINTS), F32),
            ((3 * C, C), BF16),
            ((C, C), BF16),
            ((C, POINTS), F32),
            ((TAB, 2, 1, POINTS), F32),
        ],
        (
            lat, bias_table.transpose(1, 0, 2), norm_gain.reshape(1, C), project_in, project_out,
            mask_ids.transpose(1, 0, 2),
        ),
        [((TAB, HEADS, ENTRIES), F32), ((TAB, 96, 384), F32), ((TAB, 16, 128), F32)],
        56,
    )


SUMS = [
    ((2, 2, 384, C), BF16),
    ((C, 3 * C), F32),
    ((C, C), F32),
    ((C, POINTS), F32),
    ((2 * HEADS, POINTS, POINTS), F32),
]


def run_main(me, x, y, strips, regions, gain, project_in, win_t, project_out, wout_t, bias):
    weights = (
        near(regions), near(gain), project_in, near(win_t), project_out, near(wout_t), near(bias),
    )
    x, y = near(x), near(y)
    inner = call(inner_kernel, SUMS, (x, y, *weights), [((2, 2, 15, 32, C), F32)], 48)
    return call(
        main_kernel,
        [((2, 18, 24, C), BF16)] * 2 + STRIPS[:2] + [((16, CHUNK, 128), F32), ((16, CHUNK, 128), BF16)],
        (me, x, y, *map(near, strips), *weights, *map(near, inner)),
        [
            ((2, 2, 21, 32, C), F32),
            ((C, 4 * C), F32),
            ((C, C), F32),
            ((C, POINTS), F32),
            ((TAB * HEADS, POINTS, POINTS), F32),
            ((TAB * HEADS * 16, POINTS), F32),
            ((96, 384), F32),
            ((TAB * 8, LANE_BLOCKS * 128), F32),
            ((32 * T_ROWS, 128), F32),
            ((2, 16, CHUNK, 128), F32),
        ],
        44,
    )


def local(inputs, cotangent, mask_ids, norm_gain, project_in, project_out, bias_table):
    x, y = inputs[0], cotangent[0]
    lat = lax.axis_index("lat").astype(I32).reshape(1)
    me = lax.axis_index("ens").astype(I32).reshape(1)
    *strips, x, y = call(strips_kernel, STRIPS + [((2, 18, 24, C), BF16)] * 2, (x, y), (), 56)
    strips = halo(*strips, -1)
    bias, win_t, wout_t, gain, regions = run_shadow(lat, bias_table, norm_gain, project_in, project_out, mask_ids)
    out, in_grad, lon_s, lat_s, keep, send = run_main(
        me, x, y, strips, regions, gain, project_in, win_t, project_out, wout_t, bias
    )
    got = passed(send, "ens", (2,), (1,))
    (part,) = call(over_ens_kernel, [((16, CHUNK, 128), BF16)], (near(keep), near(got)))
    part = lax.all_to_all(part, "lon", 0, 0, tiled=True)
    (part,) = call(over_lon_kernel, [((8, CHUNK, 128), BF16)], (near(part),))
    lon_s = passed(lon_s, "lon", (lax.axis_size("lon"),), (1,))
    part = lax.all_to_all(part, "lat", 0, 0, tiled=True)
    part, lat_s = call(
        over_lat_kernel,
        [((16, SHARD, 128), BF16), STRIPS[1]],
        (near(part), near(lon_s), near(lat_s)),
    )
    lat_s = passed(lat_s, "lat", (lax.axis_size("lat"),), (1,))
    mine = lax.all_to_all(part, "lon", 0, 0, tiled=True)
    mine, lat_s = lax.optimization_barrier((mine, lat_s))
    other = passed(mine, "ens", (2,), (1,))
    in_total, out_total, gain_total, table_total = call(
        final_kernel,
        [
            ((C, 3 * C), F32, None),
            ((C, C), F32, None),
            ((1, C), F32, None),
            ((HEADS, 24, ENTRIES), F32, None),
        ],
        (me, near(mine), near(other)),
        [
            ((2, 16, SHARD, 128), F32),
            ((8, 32 * T_ROWS, 128), F32),
            ((C, 4 * C), F32),
            ((144, LANE_BLOCKS * 128), F32),
        ],
    )
    out, in_grad = call(
        place_kernel,
        [((2, 18, 24, C), BF16, None)] * 2,
        (near(out), near(in_grad), near(lon_s), near(lat_s)),
    )
    return (
        out[None],
        in_grad[None],
        in_total,
        out_total,
        gain_total.reshape(C),
        table_total.transpose(1, 0, 2),
    )


def solution(mesh):
    return jax.shard_map(
        local,
        mesh=mesh,
        in_specs=(
            P("ens", None, "lat", "lon", None),
            P("ens", None, "lat", "lon", None),
            P(None, "lat", "lon"),
            P(),
            P(),
            P(),
            P(),
        ),
        out_specs=(
            P("ens", None, "lat", "lon", None),
            P("ens", None, "lat", "lon", None),
            P(),
            P(),
            P(),
            P(),
        ),
        check_vma=False,
    )
```

```python
import jax
import jax.numpy as jnp
from jax import lax
from jax.experimental import pallas as pl
from jax.experimental.pallas import tpu as pltpu
from jax.sharding import PartitionSpec as P

WL, WLAT, WLON = 2, 6, 12
AB = WL * WLAT
POINTS = AB * WLON
SPAN = 2 * WLON - 1
EPS = 1e-05
F32, BF16, I32 = jnp.float32, jnp.bfloat16, jnp.int32
C, HEADS, HD = 192, 6, 32
FACTOR = HD ** (-0.5)
TAB = 3
ENTRIES = AB * AB * SPAN
LANE_BLOCKS = -(-ENTRIES // 128)
CHUNK = 56
G_ROWS = 40
T_ROWS = 16
SHARD = 168


def dot(a, b, ca, cb):
    return lax.dot_general(a, b, (((ca,), (cb,)), ((), ())), preferred_element_type=F32)


def iota(shape, dim):
    return lax.broadcasted_iota(I32, shape, dim)


def segments():
    for ab_p in range(AB):
        a_p, b_p = divmod(ab_p, WLAT)
        for ab_r in range(AB):
            a_r, b_r = divmod(ab_r, WLAT)
            yield ab_p, ab_r, (((a_p * WL + a_r) * WLAT + b_p) * WLAT + b_r) * SPAN


def tokens():
    p = iota((1, POINTS), 1)
    c_p = (p * 21846) >> 18
    return c_p, p - c_p * AB


def toeplitz(c):
    c_p, ab_p = tokens()
    return (iota((384, POINTS), 0) == ab_p * SPAN + c_p + (WLON - 1 - c)).astype(BF16)


def heads_first():
    n = iota((96, 96), 0)
    return ((iota((96, 96), 1) == (n & 15) * 8 + (n >> 4)) & ((n & 15) < AB)).astype(BF16)


def strips_kernel(x_ref, y_ref, lon_ref, lat_ref, cor_ref, x_out, y_out):
    for k, (ref, copy) in enumerate(((x_ref, x_out), (y_ref, y_out))):
        copy[...] = ref[...]
        lon_ref[k] = ref[:, :, 0:8, :]
        lat_ref[k] = ref[:, 0:3, :, :]
        cor_ref[k] = ref[:, 0:3, 0:8, :]


def shadow_kernel(
    lat_ref, table_ref, gain_ref, win_ref, wout_ref, mask_ref,
    bias_ref, win_t_ref, wout_t_ref, gain_out, region_ref, own_ref, rows_ref, ids_ref,
):
    first = lat_ref[0] * TAB
    for t in range(TAB):
        for h in range(HEADS):
            own_ref[t, h : h + 1, :] = table_ref[h, pl.ds(first + t, 1), :]
    rows_ref[...] = jnp.zeros_like(rows_ref)
    for t in range(TAB):
        for ab_p, ab_r, start in segments():
            rows_ref[t, ab_r * 8 : ab_r * 8 + HEADS, ab_p * SPAN : (ab_p + 1) * SPAN] = own_ref[
                t, :, start : start + SPAN
            ]
    order = heads_first()
    m = iota((1, 384), 1)
    x = (m * 21846) >> 18
    swap = (iota((384, 384), 0) == (m - x * AB) * SPAN + x).astype(BF16)
    full = 0.0
    rest = [rows_ref[t] for t in range(TAB)]
    for _ in range(3):
        low = [r.astype(BF16) for r in rest]
        rest = [r - p.astype(F32) for r, p in zip(rest, low)]
        full = full + dot(jnp.concatenate([dot(order, p, 1, 0).astype(BF16) for p in low], axis=0), swap, 1, 0)
    for c in range(WLON):
        start = (WLON - 1 - c) * AB
        part = full[:, start : start + POINTS]
        for th in range(TAB * HEADS):
            bias_ref[th, c * AB : (c + 1) * AB, :] = part[th * 16 : th * 16 + AB, :]
    win_t_ref[...] = win_ref[...].T
    wout_t_ref[...] = wout_ref[...].T
    column = jnp.broadcast_to(gain_ref[...], (8, C)).T
    gain_out[...] = jnp.broadcast_to(column[:, 0:1], (C, POINTS))
    ids_ref[...] = jnp.zeros_like(ids_ref)
    c_p, ab_p = tokens()
    for v in range(TAB):
        for b in range(WLAT):
            for a in range(WL):
                at = a * WLAT + b
                ids_ref[v, at : at + 1, 0:24] = mask_ref[v * WLAT + b, a : a + 1, :].astype(F32)
        for w in range(2):
            pick = (iota((128, POINTS), 0) == c_p + WLON * w).astype(BF16)
            spread = dot(ids_ref[v].astype(BF16), pick, 1, 0)
            own = jnp.where(iota((16, POINTS), 0) == ab_p, spread, 0.0)
            region_ref[v, w] = jnp.sum(own, axis=0, keepdims=True)


def windows(weights, sums, save):
    region_ref, gain_ref, win_ref, win_t_ref, wout_ref, wout_t_ref, bias_ref = weights
    grads, outer, gain_acc = sums
    gain = gain_ref[...]
    heads = [(iota((POINTS, C), 1) >> 5) == h for h in range(HEADS)]
    c_p, ab_p = tokens()
    level = jnp.where(ab_p >= WLAT, 1, 0)
    place = (1 - level) * (WLAT * 32) + (ab_p - level * WLAT) * 32 + WLON // 2 + c_p

    def window(v, w, x_rows, y_rows):
        pick = (iota((384, POINTS), 0) == place + WLON * w).astype(BF16)
        xt = dot(x_rows, pick, 1, 0)
        ct32 = dot(y_rows, pick, 1, 0)
        yield
        ct = ct32.astype(BF16)
        center = xt - jnp.mean(xt, axis=0, keepdims=True)
        inverse = lax.rsqrt(jnp.mean(center * center, axis=0, keepdims=True) + EPS)
        part = center * inverse
        normed = (part * gain).astype(BF16)
        yield
        triple = dot(win_t_ref[...], normed, 1, 0).astype(BF16)
        grad_mixed = dot(wout_ref[...], ct, 1, 0).astype(BF16)
        yield
        natural = dot(normed, win_ref[...], 0, 0).astype(BF16)
        gm_n = dot(ct, wout_t_ref[...], 0, 0).astype(BF16)
        ids = region_ref[v, w]
        member = (iota((8, POINTS), 0).astype(F32) == ids).astype(BF16)
        barred = (dot(member, member, 0, 0) - 1.0) * 1e30
        yield
        q_n, k_n, v_n = natural[:, :C], natural[:, C : 2 * C], natural[:, 2 * C :]
        zero = jnp.zeros_like(k_n)
        k_heads = jnp.concatenate([jnp.where(m, k_n, zero) for m in heads], axis=0)
        v_heads = jnp.concatenate([jnp.where(m, v_n, zero) for m in heads], axis=0)
        all_scores = dot(k_heads, triple[:C], 1, 0)
        all_g_prob = dot(v_heads, grad_mixed, 1, 0)
        yield
        mixed, g_q, lows, g_lows = [], [], [], []
        for h in range(HEADS):
            lo, hi = h * HD, (h + 1) * HD
            part_h = slice(h * POINTS, (h + 1) * POINTS)
            scores = all_scores[part_h] * FACTOR + (bias_ref[v * HEADS + h] + barred)
            raised = jnp.exp(scores - jnp.max(scores, axis=0, keepdims=True))
            prob = raised * (1.0 / jnp.sum(raised, axis=0, keepdims=True))
            low = prob.astype(BF16)
            mixed.append(dot(triple[2 * C + lo : 2 * C + hi], low, 1, 0))
            g_prob = all_g_prob[part_h]
            g_score = prob * (g_prob - jnp.sum(prob * g_prob, axis=0, keepdims=True))
            save(v, w, h, g_score)
            g_low = g_score.astype(BF16)
            g_q.append(dot(triple[C + lo : C + hi], g_low, 1, 0) * FACTOR)
            lows.append(low)
            g_lows.append(g_low)
            yield
        all_g_v = dot(jnp.concatenate(lows, axis=0), gm_n, 1, 0)
        all_g_k = dot(jnp.concatenate(g_lows, axis=0), q_n, 1, 0)
        mixed = jnp.concatenate(mixed, axis=0).astype(BF16)
        attended = dot(wout_t_ref[...], mixed, 1, 0).astype(BF16)
        outer[...] += dot(mixed, ct, 1, 1)
        yield
        g_v, g_k = all_g_v[:POINTS], all_g_k[:POINTS]
        for h in range(1, HEADS):
            part_h = slice(h * POINTS, (h + 1) * POINTS)
            g_v = jnp.where(heads[h], all_g_v[part_h], g_v)
            g_k = jnp.where(heads[h], all_g_k[part_h], g_k)
        g_q = jnp.concatenate(g_q, axis=0).astype(BF16)
        g_k = (g_k * FACTOR).astype(BF16)
        g_v = g_v.astype(BF16)
        wide = dot(win_ref[:, :C], g_q, 1, 0)
        wide = wide + dot(win_ref[:, C : 2 * C], g_k, 1, 1) + dot(win_ref[:, 2 * C :], g_v, 1, 1)
        wide = wide.astype(BF16).astype(F32)
        yield
        grads[:, :C] += dot(normed, g_q, 1, 1)
        grads[:, C : 2 * C] += dot(normed, g_k, 1, 0)
        grads[:, 2 * C : 3 * C] += dot(normed, g_v, 1, 0)
        block = (xt + attended.astype(F32)).astype(BF16)
        gain_acc[...] += wide * part
        scaled = wide * gain
        grad_part = inverse * (
            scaled
            - jnp.mean(scaled, axis=0, keepdims=True)
            - part * jnp.mean(scaled * part, axis=0, keepdims=True)
        )
        in_grad = (ct32 + grad_part).astype(BF16)
        yield
        yield dot(pick, block, 1, 1), dot(pick, in_grad, 1, 1)

    return window


def interleaved(window, ext, chosen):
    def rows_of(k, v):
        return ext[k, :, 6 * v + 3 : 6 * v + 9].reshape(384, C).astype(BF16).T

    results = [None]
    todo = [window(v, w, rows_of(0, v), rows_of(1, v)) for v, w in chosen]
    while results[0] is None:
        results = [next(g) for g in todo]
    return dict(zip(chosen, results))


def inner_kernel(
    x_ref, y_ref, region_ref, gain_ref, win_ref, win_t_ref, wout_ref, wout_t_ref, bias_ref,
    rows_ref, grads, outer, gain_acc, dbias, ext,
):
    for k, ref in enumerate((x_ref, y_ref)):
        ext[k, :, :, 0:24, :] = ref[:, 0:15].astype(F32)
        ext[k, :, :, 24:32, :] = jnp.zeros((2, 15, 8, C), F32)
    for ref in (grads, outer, gain_acc):
        ref[...] = jnp.zeros_like(ref)

    def save(v, w, h, g_score):
        dbias[v * HEADS + h] = g_score

    weights = (region_ref, gain_ref, win_ref, win_t_ref, wout_ref, wout_t_ref, bias_ref)
    got = interleaved(windows(weights, (grads, outer, gain_acc), save), ext, [(0, 0), (1, 0)])
    for v in range(2):
        for k in range(2):
            rows_ref[k, v] = got[v, 0][k].astype(BF16)


def main_kernel(
    ens_ref, x_ref, y_ref, lon_ref, lat_ref, cor_ref, region_ref, gain_ref, win_ref, win_t_ref, wout_ref,
    wout_t_ref, bias_ref, rows_in, grads_in, outer_in, gain_in, dbias_in,
    out_ref, ig_ref, lon_out, lat_out, keep_ref, send_ref,
    ext, grads, outer, gain_acc, dbias, blocks, rows, flat_t, flat, chunks,
):
    for k, ref in enumerate((x_ref, y_ref)):
        ext[k, :, 0:18, 0:24, :] = ref[...].astype(F32)
        ext[k, :, 0:18, 24:32, :] = lon_ref[k].astype(F32)
        ext[k, :, 18:21, 0:24, :] = lat_ref[k].astype(F32)
        ext[k, :, 18:21, 24:32, :] = cor_ref[k].astype(F32)
    grads[:, : 3 * C] = grads_in[...]
    outer[...] = outer_in[...]
    gain_acc[...] = gain_in[...]

    def save(v, w, h, g_score):
        at = v * HEADS + h
        if v < 2:
            dbias[at] = dbias_in[at] + g_score
        elif w == 0:
            dbias[at] = g_score
        else:
            dbias[at] += g_score

    weights = (region_ref, gain_ref, win_ref, win_t_ref, wout_ref, wout_t_ref, bias_ref)
    got = interleaved(
        windows(weights, (grads, outer, gain_acc), save), ext, [(0, 1), (1, 1), (2, 0), (2, 1)]
    )
    for v in range(TAB):
        for k in range(2):
            first = rows_in[k, v].astype(F32) if v < 2 else got[v, 0][k]
            ext[k, :, 6 * v + 3 : 6 * v + 9] = (first + got[v, 1][k]).reshape(2, 6, 32, C)
    for k, ref in enumerate((out_ref, ig_ref)):
        ext[k, :, 0:3] = jnp.zeros((2, 3, 32, C), F32)
        ref[...] = ext[k, :, 0:18, 0:24, :].astype(BF16)
        lon_out[k] = ext[k, :, 3:21, 24:32, :].astype(BF16)
        lat_out[k] = ext[k, :, 18:21, 0:24, :].astype(BF16)

    blocks[...] = jnp.zeros_like(blocks)
    total = jnp.zeros((TAB * HEADS * 16, 384), F32)
    for c in range(WLON):
        for th in range(TAB * HEADS):
            blocks[th * 16 : th * 16 + AB, :] = dbias[th, c * AB : (c + 1) * AB, :]
        total = total + dot(blocks[...].astype(BF16), toeplitz(c), 1, 1)
    flat_t[...] = jnp.zeros_like(flat_t)
    for t in range(TAB):
        rows[...] = dot(heads_first(), total[t * 96 : (t + 1) * 96].astype(BF16), 0, 0)
        for ab_p, ab_r, start in segments():
            flat_t[t * 8 : t * 8 + 8, start : start + SPAN] = rows[
                ab_r * 8 : ab_r * 8 + 8, ab_p * SPAN : (ab_p + 1) * SPAN
            ]
    flat[...] = jnp.zeros_like(flat)
    for block in range(LANE_BLOCKS):
        for t in range(TAB):
            at = (block * TAB + t) * HEADS
            flat[at : at + HEADS, :] = flat_t[t * 8 : t * 8 + HEADS, block * 128 : (block + 1) * 128]

    chunks[...] = jnp.zeros_like(chunks)
    grads[:, 3 * C :] = outer[...]
    tile = 0
    for group in range(C // 8):
        for block in range(C * 4 // 128):
            chunk, slot = divmod(tile, G_ROWS // 8)
            chunks[chunk // 16, chunk % 16, slot * 8 : slot * 8 + 8, :] = grads[
                group * 8 : group * 8 + 8, block * 128 : (block + 1) * 128
            ]
            tile += 1
    for chunk in range(32):
        chunks[chunk // 16, chunk % 16, G_ROWS : G_ROWS + T_ROWS, :] = flat[chunk * T_ROWS : (chunk + 1) * T_ROWS]
    rest = gain_acc[...]
    gain_row = jnp.zeros((8, C), F32)
    for _ in range(3):
        low = rest.astype(BF16)
        rest = rest - low.astype(F32)
        gain_row = gain_row + dot(jnp.ones((8, POINTS), BF16), low, 1, 1)
    chunks[1, 13, 0:1, :] = gain_row[0:1, 0:128]
    chunks[1, 13, 1:2, 0:64] = gain_row[0:1, 128:192]
    me = ens_ref[0]
    keep_ref[...] = chunks[me]
    send_ref[...] = chunks[1 - me].astype(BF16)


def over_ens_kernel(keep_ref, got_ref, out_ref):
    out_ref[...] = (keep_ref[...] + got_ref[...].astype(F32)).astype(BF16)


def over_lon_kernel(got_ref, out_ref):
    total = jnp.sum(got_ref[...].astype(F32), axis=0).astype(BF16)
    for k in range(out_ref.shape[0]):
        out_ref[k] = total


def over_lat_kernel(got_ref, lon_ref, lat_ref, out_ref, lat_out):
    lat_out[:, :, :, 8:24, :] = lat_ref[:, :, :, 8:24, :]
    corner = lat_ref[:, :, :, 0:8, :].astype(F32) + lon_ref[:, :, 15:18].astype(F32)
    lat_out[:, :, :, 0:8, :] = corner.astype(BF16)
    got = got_ref[...].astype(F32)
    total = jnp.sum(got[:, :G_ROWS], axis=0)
    shard = jnp.concatenate([total] + [got[k, G_ROWS : G_ROWS + T_ROWS] for k in range(8)], axis=0).astype(BF16)
    for k in range(out_ref.shape[0]):
        out_ref[k] = shard


def place_kernel(out_ref, grad_ref, lon_ref, lat_ref, out_whole, grad_whole):
    for k, (ref, whole) in enumerate(((out_ref, out_whole), (grad_ref, grad_whole))):
        left = ref[:, 3:, 0:8, :].astype(F32) + lon_ref[k, :, 0:15].astype(F32)
        whole[:, 3:, 0:8, :] = left.astype(BF16)
        whole[:, 3:, 8:24, :] = ref[:, 3:, 8:24, :]
        whole[:, 0:3] = lat_ref[k]


def final_kernel(ens_ref, mine_ref, other_ref, in_ref, outer_ref, gain_ref, table_ref, both, tables, grads, full):
    me = ens_ref[0]
    both[me] = mine_ref[...].astype(F32)
    both[1 - me] = other_ref[...].astype(F32)
    tile = 0
    for group in range(C // 8):
        for block in range(C * 4 // 128):
            chunk, slot = divmod(tile, G_ROWS // 8)
            grads[group * 8 : group * 8 + 8, block * 128 : (block + 1) * 128] = both[
                chunk // 16, chunk % 16, slot * 8 : slot * 8 + 8, :
            ]
            tile += 1
    in_ref[...] = grads[:, 0 : 3 * C]
    outer_ref[...] = grads[:, 3 * C :]
    gain_ref[0:1, 0:128] = both[1, 13, 0:1, :]
    gain_ref[0:1, 128:192] = both[1, 13, 1:2, 0:64]
    for lat in range(8):
        for chunk in range(32):
            tables[lat, chunk * T_ROWS : (chunk + 1) * T_ROWS, :] = both[
                chunk // 16, chunk % 16, G_ROWS + lat * T_ROWS : G_ROWS + (lat + 1) * T_ROWS, :
            ]
    count = TAB * HEADS
    for lat in range(8):
        for block in range(LANE_BLOCKS):
            full[lat * count : (lat + 1) * count, block * 128 : (block + 1) * 128] = tables[
                lat, block * count : (block + 1) * count, :
            ]
    m = iota((144, 144), 0)
    h24 = (m * 43691) >> 20
    order = (iota((144, 144), 1) == (m - h24 * 24) * HEADS + h24).astype(BF16)
    ordered = dot(order, full[...].astype(BF16), 1, 0)
    for h in range(HEADS):
        table_ref[h] = ordered[h * 24 : (h + 1) * 24, :ENTRIES]


SMEM = pl.BlockSpec(memory_space=pltpu.SMEM)
WHOLE = pl.BlockSpec(memory_space=pltpu.VMEM)


def call(kernel, outs, args, scratch=(), room=24):
    specs = [SMEM if a.dtype == I32 and a.ndim == 1 else WHOLE for a in args]
    shapes = tuple(pltpu.VMEM(*o) if len(o) == 2 else jax.ShapeDtypeStruct(*o[:2]) for o in outs)
    return pl.pallas_call(
        kernel,
        out_shape=shapes,
        in_specs=specs,
        out_specs=tuple(WHOLE for _ in outs),
        scratch_shapes=[pltpu.VMEM(*x) for x in scratch],
        compiler_params=pltpu.CompilerParams(vmem_limit_bytes=room * 2**20),
    )(*args)


def near(x):
    return pltpu.with_memory_space_constraint(x, pltpu.VMEM)


def passed(x, axes, sizes, moves):
    total = [()]
    for size in sizes:
        total = [t + (i,) for t in total for i in range(size)]

    def number(index):
        n = 0
        for i, size in zip(index, sizes):
            n = n * size + i % size
        return n

    pairs = [(number(t), number(tuple(i + m for i, m in zip(t, moves)))) for t in total]
    return lax.ppermute(x, axes, pairs)


def halo(lon_strip, lat_strip, corner, by):
    n_lon, n_lat = lax.axis_size("lon"), lax.axis_size("lat")
    return (
        passed(lon_strip, "lon", (n_lon,), (by,)),
        passed(lat_strip, "lat", (n_lat,), (by,)),
        passed(corner, ("lon", "lat"), (n_lon, n_lat), (by, by)),
    )


STRIPS = [((2, 2, 18, 8, C), BF16), ((2, 2, 3, 24, C), BF16), ((2, 2, 3, 8, C), BF16)]


def run_shadow(lat, bias_table, norm_gain, project_in, project_out, mask_ids):
    return call(
        shadow_kernel,
        [
            ((TAB * HEADS, POINTS, POINTS), F32),
            ((3 * C, C), BF16),
            ((C, C), BF16),
            ((C, POINTS), F32),
            ((TAB, 2, 1, POINTS), F32),
        ],
        (
            lat, bias_table.transpose(1, 0, 2), norm_gain.reshape(1, C), project_in, project_out,
            mask_ids.transpose(1, 0, 2),
        ),
        [((TAB, HEADS, ENTRIES), F32), ((TAB, 96, 384), F32), ((TAB, 16, 128), F32)],
        56,
    )


SUMS = [
    ((2, 2, 384, C), BF16),
    ((C, 3 * C), F32),
    ((C, C), F32),
    ((C, POINTS), F32),
    ((2 * HEADS, POINTS, POINTS), F32),
]


def run_main(me, x, y, strips, regions, gain, project_in, win_t, project_out, wout_t, bias):
    weights = (
        near(regions), near(gain), project_in, near(win_t), project_out, near(wout_t), near(bias),
    )
    x, y = near(x), near(y)
    inner = call(inner_kernel, SUMS, (x, y, *weights), [((2, 2, 15, 32, C), F32)], 48)
    return call(
        main_kernel,
        [((2, 18, 24, C), BF16)] * 2 + STRIPS[:2] + [((16, CHUNK, 128), F32), ((16, CHUNK, 128), BF16)],
        (me, x, y, *map(near, strips), *weights, *map(near, inner)),
        [
            ((2, 2, 21, 32, C), F32),
            ((C, 4 * C), F32),
            ((C, C), F32),
            ((C, POINTS), F32),
            ((TAB * HEADS, POINTS, POINTS), F32),
            ((TAB * HEADS * 16, POINTS), F32),
            ((96, 384), F32),
            ((TAB * 8, LANE_BLOCKS * 128), F32),
            ((32 * T_ROWS, 128), F32),
            ((2, 16, CHUNK, 128), F32),
        ],
        44,
    )


def local(inputs, cotangent, mask_ids, norm_gain, project_in, project_out, bias_table):
    x, y = inputs[0], cotangent[0]
    lat = lax.axis_index("lat").astype(I32).reshape(1)
    me = lax.axis_index("ens").astype(I32).reshape(1)
    *strips, x, y = call(strips_kernel, STRIPS + [((2, 18, 24, C), BF16)] * 2, (x, y), (), 56)
    strips = halo(*strips, -1)
    bias, win_t, wout_t, gain, regions = run_shadow(lat, bias_table, norm_gain, project_in, project_out, mask_ids)
    out, in_grad, lon_s, lat_s, keep, send = run_main(
        me, x, y, strips, regions, gain, project_in, win_t, project_out, wout_t, bias
    )
    got = passed(send, "ens", (2,), (1,))
    (part,) = call(over_ens_kernel, [((16, CHUNK, 128), BF16)], (near(keep), near(got)))
    part = lax.all_to_all(part, "lon", 0, 0, tiled=True)
    (part,) = call(over_lon_kernel, [((8, CHUNK, 128), BF16)], (near(part),))
    lon_s = passed(lon_s, "lon", (lax.axis_size("lon"),), (1,))
    part = lax.all_to_all(part, "lat", 0, 0, tiled=True)
    part, lat_s = call(
        over_lat_kernel,
        [((16, SHARD, 128), BF16), STRIPS[1]],
        (near(part), near(lon_s), near(lat_s)),
    )
    lat_s = passed(lat_s, "lat", (lax.axis_size("lat"),), (1,))
    mine = lax.all_to_all(part, "lon", 0, 0, tiled=True)
    mine, lat_s = lax.optimization_barrier((mine, lat_s))
    other = passed(mine, "ens", (2,), (1,))
    in_total, out_total, gain_total, table_total = call(
        final_kernel,
        [
            ((C, 3 * C), F32, None),
            ((C, C), F32, None),
            ((1, C), F32, None),
            ((HEADS, 24, ENTRIES), F32, None),
        ],
        (me, near(mine), near(other)),
        [
            ((2, 16, SHARD, 128), F32),
            ((8, 32 * T_ROWS, 128), F32),
            ((C, 4 * C), F32),
            ((144, LANE_BLOCKS * 128), F32),
        ],
    )
    out, in_grad = call(
        place_kernel,
        [((2, 18, 24, C), BF16, None)] * 2,
        (near(out), near(in_grad), near(lon_s), near(lat_s)),
    )
    return (
        out[None],
        in_grad[None],
        in_total,
        out_total,
        gain_total.reshape(C),
        table_total.transpose(1, 0, 2),
    )


def solution(mesh):
    return jax.shard_map(
        local,
        mesh=mesh,
        in_specs=(
            P("ens", None, "lat", "lon", None),
            P("ens", None, "lat", "lon", None),
            P(None, "lat", "lon"),
            P(),
            P(),
            P(),
            P(),
        ),
        out_specs=(
            P("ens", None, "lat", "lon", None),
            P("ens", None, "lat", "lon", None),
            P(),
            P(),
            P(),
            P(),
        ),
        check_vma=False,
    )
```
